32 devices in a mesh: row: 8 (over y, x, core), col: 4 (over z).
Axes of the slice: x: 2, y: 2, z: 4, core: 2. Of those that a mesh axis runs over, the one named last changes fastest.
Arguments:
- blocks: bfloat16 [8, 4, 64, 128, 128], P('row', 'col'), may hold values from -0.046875 to 0.046875
- block_rows: int32 [8, 4, 64], P('row', 'col'), may hold values from 0 to 7, as said below
- block_cols: int32 [8, 4, 64], P('row', 'col'), may hold values from 0 to 15, as said below
- block_count: int32 [8, 4], P('row', 'col'), may hold values from 16 to 64, as said below
- probes: float32 [64, 8192], P(None, ('row', 'col')), may hold values from -6 to 6
- t_prev: float32 [64, 8192], P(None, ('row', 'col')), may hold values from -6 to 6
- t_cur: float32 [64, 8192], P(None, ('row', 'col')), may hold values from -6 to 6
- accum: float32 [64, 8192], P(None, ('row', 'col')), may hold values from -6 to 6
- coeffs: float32 [2], replicated, may hold values from 0.5 to 1.5
Outputs:
- t_next: float32 [64, 8192], P(None, ('row', 'col'))
- t_after: float32 [64, 8192], P(None, ('row', 'col'))
- accum_out: float32 [64, 8192], P(None, ('row', 'col'))
- moments: float32 [2, 64], replicated
The draws below stay inside these ranges and needn't reach their ends.
Inputs may be any that keep to these rules, and one draw needn't show every extreme that they name: `block_rows`: within one device the live slots name distinct blocks; block rows lie in [0, 8) and block columns in [0, 16). `block_cols`: pairs with block_rows: within one device the live slots name distinct blocks. `block_count`: some device has all 64 slots live in every draw.
All inputs are finite; a program needn't handle non-finite values.
Results may differ from the reference program's by a relative error of at most 0.0025.
Values may be sent and summed in bfloat16 or wider, within the bound.
No kernel may reach another device: no remote copies, remote signals or barrier semaphores. Data moves between devices by JAX's collectives and lax.ppermute only.
A program may use at most 64 MiB of HBM per device.

```python
import jax
import jax.numpy as jnp
from jax import lax

BS = 128
PROBES = 64
PB = 2
SLOTS_ROW = 8
LROWS = 8
LCOLS = 16
MAXB = 64
ORDER = 8192
N_ROW = 8
N_COL = 4


def pattern_places(key):
    grid_rows = LCOLS // PB
    grid_cols = LROWS // PB
    sub_keys = jax.random.split(jax.random.fold_in(key, 17), grid_rows * grid_cols)

    def device_slots(sub_key):
        return jax.random.permutation(sub_key, LROWS * LCOLS)[:MAXB]
    places = jax.vmap(device_slots)(sub_keys)
    return places.reshape(grid_rows, grid_cols, MAXB).astype(jnp.int32)


def draw_block_rows(key, part):
    return (pattern_places(key) // LCOLS).astype(jnp.int32)


def draw_block_cols(key, part):
    return (pattern_places(key) % LCOLS).astype(jnp.int32)


def draw_block_count(key, part):
    grid_rows = LCOLS // PB
    grid_cols = LROWS // PB
    devices_all = grid_rows * grid_cols
    drawn = jax.random.randint(jax.random.fold_in(key, 29), (devices_all,), MAXB // 4, MAXB + 1)
    fullest = jax.random.randint(jax.random.fold_in(key, 31), (), 0, devices_all)
    drawn = jnp.where(jnp.arange(devices_all) == fullest, MAXB, drawn)
    return drawn.reshape(grid_rows, grid_cols).astype(jnp.int32)


def block_levels(key, extent, shards, least, largest):
    loudness, own = 1.0, jax.random.fold_in(key, 6)
    for position, blocks in shards:
        draws = jnp.exp(jax.random.uniform(jax.random.fold_in(own, position), (blocks,), jnp.float32, least / len(shards), largest / len(shards)))
        loudness = loudness * jnp.repeat(draws, extent[position] // blocks).reshape([-1 if axis == position else 1 for axis in range(len(extent))])
    return loudness


def bell_draw(key, shape, spread, limit, pieces=(), held_as=jnp.bfloat16):
    entries = jax.random.normal(key, shape, jnp.float32) * spread
    if len(pieces) > 0:
        entries = block_levels(key, shape, pieces, -0.22, 0.18) * entries
    return jnp.clip(entries, min=-limit, max=limit).astype(held_as)


def setup_inputs(seed: int = 0) -> dict:
    key_list = jax.random.split(jax.random.key(seed), 10)
    return {
        "blocks": bell_draw(key_list[0], (N_ROW, N_COL, MAXB, BS, BS), (4 * BS * N_COL * SLOTS_ROW) ** -0.5, 0.046875, ((0, 8), (1, 4))),
        "block_rows": draw_block_rows(jax.random.fold_in(key_list[9], 71), 0),
        "block_cols": draw_block_cols(jax.random.fold_in(key_list[9], 71), 0),
        "block_count": draw_block_count(jax.random.fold_in(key_list[9], 71), 0),
        "probes": bell_draw(key_list[4], (PROBES, ORDER), 1.0, 6.0, ((1, 32),), jnp.float32),
        "t_prev": bell_draw(key_list[5], (PROBES, ORDER), 1.0, 6.0, ((1, 32),), jnp.float32),
        "t_cur": bell_draw(key_list[6], (PROBES, ORDER), 1.0, 6.0, ((1, 32),), jnp.float32),
        "accum": bell_draw(key_list[7], (PROBES, ORDER), 1.0, 6.0, ((1, 32),), jnp.float32),
        "coeffs": jnp.clip(jax.random.uniform(key_list[8], (2,), jnp.float32, 0.5, 1.5), 0.5, 1.5),
    }


def product(blocks, block_rows, block_cols, block_count, vectors):
    split_vec = vectors.astype(jnp.bfloat16).reshape(PROBES, N_ROW, N_COL, PB * BS)
    slot_ids = jnp.arange(MAXB, dtype=jnp.int32)

    def per_row(row_idx):
        def per_col(total, col_idx):
            column_set = lax.dynamic_index_in_dim(split_vec, col_idx, 2, keepdims=False)
            column_set = column_set.reshape(PROBES, LCOLS, BS)
            tiles = blocks[row_idx, col_idx].astype(jnp.float32)
            row_ids = block_rows[row_idx, col_idx]
            col_ids = block_cols[row_idx, col_idx]
            alive = (slot_ids < block_count[row_idx, col_idx]).astype(jnp.float32)
            picked = jnp.take(column_set, col_ids, axis=1).astype(jnp.float32)
            contrib = jnp.einsum("pgj,gij->pgi", picked, tiles) * alive[None, :, None]
            partial_value = jnp.zeros((PROBES, LROWS, BS), jnp.float32).at[:, row_ids, :].add(contrib)
            return total + partial_value, None

        start = jnp.zeros((PROBES, LROWS, BS), jnp.float32)
        total, _ = lax.scan(per_col, start, jnp.arange(N_COL, dtype=jnp.int32))
        return total.reshape(PROBES, LROWS * BS)

    row_sets = lax.map(per_row, jnp.arange(N_ROW, dtype=jnp.int32))
    return jnp.transpose(row_sets, (1, 0, 2)).reshape(PROBES, ORDER)


def reference(blocks, block_rows, block_cols, block_count, probes, t_prev, t_cur, accum, coeffs):
    t_next = 2.0 * product(blocks, block_rows, block_cols, block_count, t_cur) - t_prev
    t_after = 2.0 * product(blocks, block_rows, block_cols, block_count, t_next) - t_cur
    accum_out = accum + coeffs[0] * t_next + coeffs[1] * t_after
    scale = float(ORDER) ** -0.5
    first = jnp.sum(probes * t_next, axis=1) * scale
    second = jnp.sum(probes * t_after, axis=1) * scale
    moments = jnp.stack([first, second])
    return t_next, t_after, accum_out, moments
```

```python
import functools

import jax
import jax.numpy as jnp
from jax import lax
from jax.experimental import pallas as pl
from jax.experimental.pallas import tpu as pltpu
from jax.sharding import PartitionSpec as P

VMEM = pl.BlockSpec(memory_space=pltpu.VMEM)
SMEM = pl.BlockSpec(memory_space=pltpu.SMEM)
HBM = pl.BlockSpec(memory_space=pltpu.HBM)
CONTRACT_LAST = (((1,), (1,)), ((), ()))
F32, BF16 = jnp.float32, jnp.bfloat16
LANES = 128


def place_kernel(pb, group, count, rows_in, cols_in, blocks, dense, held, rows, cols, sems, own_sems):
    r, c = lax.axis_index("row"), lax.axis_index("col")
    bs = blocks.shape[-1]
    groups = held.shape[0] // group

    def fetch(g):
        span = pl.ds(g * group, group)
        return pltpu.make_async_copy(blocks.at[0, 0, span], held.at[span], sems.at[g])

    names = (
        pltpu.make_async_copy(rows_in, rows, own_sems.at[0]),
        pltpu.make_async_copy(cols_in, cols, own_sems.at[1]),
    )
    for copy in names:
        copy.start()
    for g in range(groups):
        fetch(g).start()
    dense[...] = jnp.zeros_like(dense)
    for copy in names:
        copy.wait()
    live = count[0, 0]

    def put(slot):
        @pl.when(slot < live)
        def _():
            i, j = rows[0, 0, slot], cols[0, 0, slot]
            line = ((i // pb) ^ c) * pb + i % pb
            dense[(j // pb) ^ r, j % pb, pl.ds(pl.multiple_of(line * bs, bs), bs), :] = held[slot]

    for g in range(groups):
        fetch(g).wait()
        for n in range(group):
            put(g * group + n)


def dots(pb, order, vectors, dense, m, width):
    total = None
    for h, k in enumerate(order):
        w = jnp.concatenate([dense[k, s, pl.ds(m * width, width), :] for s in range(pb)], axis=1)
        part = lax.dot_general(vectors[h], w, CONTRACT_LAST, preferred_element_type=F32)
        total = part if total is None else total + part
    return total


def first_half_kernel(pb, order, vectors, dense, out):
    width = vectors.shape[2]
    for m in range(out.shape[0]):
        out[m] = dots(pb, order, vectors, dense, m, width)


def as_row(column):
    n = column.shape[0]
    shape = (n, LANES)
    here = lax.broadcasted_iota(jnp.int32, shape, 0) == lax.broadcasted_iota(jnp.int32, shape, 1)
    return jnp.sum(jnp.where(here, column, 0.0), axis=0, keepdims=True)


def two_parts(x):
    high = x.astype(BF16).astype(F32)
    return high, x - high


def second_half_kernel(pb, order, n_probes, vectors, dense, half, *refs):
    width = vectors.shape[2]
    chunks = half.shape[0]
    tile = None
    if n_probes:
        before, probes, refs = refs[0], refs[1 : 1 + n_probes], refs[1 + n_probes :]
    own, sends = refs[0], refs[1 : chunks]
    sums = None
    for m in range(chunks):
        total = half[m] + dots(pb, order, vectors, dense, m, width)
        if n_probes:
            part = jnp.sum(probes[m][...] * total, axis=1, keepdims=True)
            sums = part if sums is None else sums + part
        if m == 0:
            own[...] = total
        else:
            sends[m - 1][pl.ds(0, total.shape[0]), :] = total.astype(BF16)[:, :LANES]
            for s in range(1, width // LANES):
                sends[m - 1][pl.ds(s * total.shape[0], total.shape[0]), :] = total.astype(BF16)[
                    :, s * LANES : (s + 1) * LANES
                ]
    if n_probes:
        tile_out = refs[chunks]
        both = before[...][:2] + jnp.concatenate([jnp.zeros((1, LANES), F32), 2.0 * as_row(sums)], axis=0)
        tile_out[...] = jnp.concatenate([both, jnp.zeros((6, LANES), F32)], axis=0)
        high, low = two_parts(both)
        tile = jnp.concatenate([high, low, jnp.zeros((12, LANES), F32)], axis=0).astype(BF16)
        for m in range(1, chunks):
            sends[m - 1][pl.ds(width // LANES * own.shape[0], 16), :] = tile


def gathered(own, received):
    count, width = own.shape
    total = own[...]
    for r in received:
        piece = jnp.concatenate(
            [r[pl.ds(s * count, count), :] for s in range(width // LANES)], axis=1
        )
        total = total + piece.astype(F32)
    return total


def next_kernel(n_col, own, *refs):
    received, (prev, cur, probes, rounded, tile) = refs[: n_col - 1], refs[n_col - 1 :]
    value = 2.0 * gathered(own, received) - prev[...]
    rounded[...] = value.astype(BF16)
    ahead = as_row(jnp.sum(probes[...] * value, axis=1, keepdims=True))
    back = as_row(jnp.sum(probes[...] * cur[...], axis=1, keepdims=True))
    tile[...] = jnp.concatenate([ahead, -back, jnp.zeros((6, LANES), F32)], axis=0)


def value_kernel(n_col, own, *refs):
    received, (prev, out) = refs[: n_col - 1], refs[n_col - 1 :]
    out[...] = 2.0 * gathered(own, received) - prev[...]


def tile_kernel(start, mine, *refs):
    received, tile = refs[:-1], refs[-1]
    total = mine[...]
    for r in received:
        t = r[pl.ds(start, 16), :].astype(F32)
        total = total + jnp.concatenate([t[0:2] + t[2:4], jnp.zeros((6, LANES), F32)], axis=0)
    tile[...] = total


def last_kernel(n_col, coeffs, own, *refs):
    received = refs[: n_col - 1]
    prev, t_next, accum, t_after, accum_out = refs[n_col - 1 :]
    value = 2.0 * gathered(own, received) - prev[...]
    t_after[...] = value
    accum_out[...] = accum[...] + coeffs[0] * t_next[...] + coeffs[1] * value


def local(n_row, n_col, blocks, block_rows, block_cols, block_count, probes, t_prev, t_cur, accum, coeffs):
    n_slots, bs = blocks.shape[2], blocks.shape[-1]
    count, width = t_cur.shape
    pb = width // bs
    total_rows = width * n_row * n_col
    dense_bytes = n_row * n_col * width * width * 2
    params = pltpu.CompilerParams(vmem_limit_bytes=min(60 * 1024 * 1024, 3 * dense_bytes))
    barrier = lax.optimization_barrier

    def swap(x, axis, k):
        n = n_row if axis == "row" else n_col
        return lax.ppermute(x, axis, [(i, i ^ k) for i in range(n)])

    def call(kernel, out_shape, in_specs, name, **more):
        one = not isinstance(out_shape, list)
        return pl.pallas_call(
            kernel,
            out_shape=out_shape,
            in_specs=in_specs,
            out_specs=VMEM if one else [VMEM] * len(out_shape),
            compiler_params=params,
            name=name,
            **more,
        )

    def in_hbm(x):
        return pltpu.with_memory_space_constraint(x, pltpu.HBM)

    def shape(*dims, dtype=F32):
        return jax.ShapeDtypeStruct(dims, dtype)

    group = 8
    dense = call(
        functools.partial(place_kernel, pb, group),
        shape(n_row, pb, n_col * width, bs, dtype=BF16),
        [SMEM] + [HBM] * 3,
        "place",
        scratch_shapes=[
            pltpu.VMEM((n_slots, bs, bs), BF16),
            pltpu.SMEM(block_rows.shape, jnp.int32),
            pltpu.SMEM(block_cols.shape, jnp.int32),
            pltpu.SemaphoreType.DMA((n_slots // group,)),
            pltpu.SemaphoreType.DMA((2,)),
        ],
    )(block_count, *(in_hbm(x) for x in (block_rows, block_cols, blocks)))

    far = list(range(n_row - 2, 0, -2))
    mine_order = [0] + [k ^ 1 for k in far]
    others_order = [1] + far

    def gather(v):
        got = [swap(v, "row", k ^ 1) for k in far]
        head, tail = jnp.stack([v] + got[:-1]), got[-1][None]
        return head, tail

    send_rows = width // LANES * count

    def halves(head, tail, dense, extra, name):
        other = [swap(head, "row", 1), swap(tail, "row", 1)]
        mine = jnp.concatenate([head, tail])
        half = call(
            functools.partial(first_half_kernel, pb, mine_order),
            shape(n_col, count, width),
            [VMEM] * 2,
            name + "_a",
        )(mine, dense)
        others = jnp.concatenate(other)
        n_probes = n_col if extra else 0
        outs = [shape(count, width)]
        outs += [shape(send_rows + (16 if extra else 0), LANES, dtype=BF16)] * (n_col - 1)
        if extra:
            outs.append(shape(8, LANES))
        return call(
            functools.partial(second_half_kernel, pb, others_order, n_probes),
            outs,
            [VMEM] * (3 + (1 + n_probes if extra else 0)),
            name + "_b",
        )(others, dense, half, *(extra or []))

    reduce_order = [2, 1, 3] if n_col == 4 else list(range(1, n_col))

    def exchange(sends):
        got = {m: swap(sends[m - 1], "col", m) for m in reduce_order}
        return [got[m] for m in reduce_order]

    head, tail = gather(barrier(t_cur.astype(BF16)))
    probe_pieces = {0: probes}
    stages = [n_col >> (i + 1) for i in range(n_col.bit_length() - 1)]
    k = stages[0]
    probe_pieces[k] = swap(probes, "col", k)
    head, tail, dense = barrier((head, tail, dense))
    own, *sends = halves(head, tail, dense, None, "first")
    received = exchange(sends)
    rounded, tile = call(
        functools.partial(next_kernel, n_col),
        [shape(count, width, dtype=BF16), shape(8, LANES)],
        [VMEM] * (n_col + 3),
        "next",
    )(own, *received, t_prev, t_cur, probes)
    t_next = call(
        functools.partial(value_kernel, n_col), shape(count, width), [VMEM] * (n_col + 1), "value"
    )(own, *received, t_prev)

    head, tail = gather(rounded)
    rounded, probe_pieces = barrier((rounded, probe_pieces))
    for k in stages[1:]:
        keys = list(probe_pieces)
        got = swap(jnp.stack([probe_pieces[m] for m in keys]), "col", k)
        for n, m in enumerate(keys):
            probe_pieces[m ^ k] = got[n]
    extra = [tile] + [probe_pieces[m] for m in range(n_col)]
    own, *sends, mine = halves(head, tail, dense, extra, "second")
    received = exchange(sends)
    tile = call(
        functools.partial(tile_kernel, send_rows), shape(8, LANES), [VMEM] * n_col, "sums"
    )(mine, *received)
    t_after, accum_out = call(
        functools.partial(last_kernel, n_col),
        [shape(count, width), shape(count, width)],
        [SMEM] + [VMEM] * (n_col + 3),
        "last",
    )(coeffs, own, *received, t_cur, t_next, accum)

    total = tile
    for k in far:
        total = total + swap(tile, "row", k ^ 1)
    total = total + swap(total, "row", 1)
    moments = total[:2, :count] * float(total_rows) ** (-0.5)
    return (t_next, t_after, accum_out, moments)


def solution(mesh):
    vector = P(None, ("row", "col"))
    return jax.shard_map(
        functools.partial(local, mesh.shape["row"], mesh.shape["col"]),
        mesh=mesh,
        in_specs=(
            P("row", "col", None, None, None),
            P("row", "col", None),
            P("row", "col", None),
            P("row", "col"),
            vector,
            vector,
            vector,
            vector,
            P(),
        ),
        out_specs=(vector, vector, vector, P()),
        check_vma=False,
    )
```

```python
import functools

import jax
import jax.numpy as jnp
from jax import lax
from jax.experimental import pallas as pl
from jax.experimental.pallas import tpu as pltpu
from jax.sharding import PartitionSpec as P

VMEM = pl.BlockSpec(memory_space=pltpu.VMEM)
SMEM = pl.BlockSpec(memory_space=pltpu.SMEM)
HBM = pl.BlockSpec(memory_space=pltpu.HBM)
CONTRACT_LAST = (((1,), (1,)), ((), ()))
F32, BF16 = jnp.float32, jnp.bfloat16
LANES = 128
ORDER1 = [1, 3, 2]
ORDER2 = [2, 3, 1]
FAR = [6, 4, 2]


def place_kernel(pb, group, count, rows_in, cols_in, blocks, dense, held, rows, cols, sems, own_sems):
    r, c = lax.axis_index("row"), lax.axis_index("col")
    bs = blocks.shape[-1]
    groups = held.shape[0] // group

    def fetch(g):
        span = pl.ds(g * group, group)
        return pltpu.make_async_copy(blocks.at[0, 0, span], held.at[span], sems.at[g])

    names = (
        pltpu.make_async_copy(rows_in, rows, own_sems.at[0]),
        pltpu.make_async_copy(cols_in, cols, own_sems.at[1]),
    )
    for copy in names:
        copy.start()
    for g in range(groups):
        fetch(g).start()
    dense[...] = jnp.zeros_like(dense)
    for copy in names:
        copy.wait()
    live = count[0, 0]

    def put(slot):
        @pl.when(slot < live)
        def _():
            i, j = rows[0, 0, slot], cols[0, 0, slot]
            line = ((i // pb) ^ c) * pb + i % pb
            dense[(j // pb) ^ r, j % pb, pl.ds(pl.multiple_of(line * bs, bs), bs), :] = held[slot]

    for g in range(groups):
        fetch(g).wait()
        for n in range(group):
            put(g * group + n)


def dots(pb, order, vectors, dense, m, width):
    total = None
    for h, k in enumerate(order):
        w = jnp.concatenate([dense[k, s, pl.ds(m * width, width), :] for s in range(pb)], axis=1)
        part = lax.dot_general(vectors[h], w, CONTRACT_LAST, preferred_element_type=F32)
        total = part if total is None else total + part
    return total


def first_half_kernel(pb, order, vectors, dense, out):
    width = vectors.shape[2]
    for m in range(out.shape[0]):
        out[m] = dots(pb, order, vectors, dense, m, width)


def as_row(column):
    n = column.shape[0]
    shape = (n, LANES)
    here = lax.broadcasted_iota(jnp.int32, shape, 0) == lax.broadcasted_iota(jnp.int32, shape, 1)
    return jnp.sum(jnp.where(here, column, 0.0), axis=0, keepdims=True)


def two_parts(x):
    high = x.astype(BF16).astype(F32)
    return high, x - high


def put_halves(ref, start, value):
    count = value.shape[0]
    for s in range(value.shape[1] // LANES):
        ref[pl.ds(start + s * count, count), :] = value[:, s * LANES : (s + 1) * LANES]


def get_halves(ref, start, count, width):
    return jnp.concatenate(
        [ref[pl.ds(start + s * count, count), :] for s in range(width // LANES)], axis=1
    )


def second_half_kernel(pb, order, send_order, n_carried, vectors, dense, half, *refs):
    width, chunks = vectors.shape[2], half.shape[0]
    carried, own = refs[:n_carried], refs[n_carried]
    sends = dict(zip(send_order, refs[n_carried + 1 :]))
    for m in range(chunks):
        total = half[m] + dots(pb, order, vectors, dense, m, width)
        if m == 0:
            own[...] = total
        else:
            put_halves(sends[m], 0, total.astype(BF16))
    rows = own.shape[0] * width // LANES
    for n, piece in enumerate(carried):
        put_halves(sends[1], (n + 1) * rows, piece[...].astype(BF16))


def second_half_moment_kernel(pb, order, send_order, n_kept, vectors, dense, half, before, message, *refs):
    width, chunks = vectors.shape[2], half.shape[0]
    kept, own, tile_out = refs[:n_kept], refs[n_kept], refs[-1]
    sends = dict(zip(send_order, refs[n_kept + 1 : -1]))
    count = own.shape[0]
    rows = count * width // LANES
    sums = None
    for m in range(chunks):
        total = half[m] + dots(pb, order, vectors, dense, m, width)
        if m % 2:
            probes = get_halves(message, m // 2 * rows, count, width).astype(F32)
        else:
            probes = kept[m // 2][...].astype(F32)
        part = jnp.sum(probes * total, axis=1, keepdims=True)
        sums = part if sums is None else sums + part
        if m == 0:
            own[...] = total
        else:
            put_halves(sends[m], 0, total.astype(BF16))
    both = before[...][:2] + jnp.concatenate([jnp.zeros((1, LANES), F32), 2.0 * as_row(sums)], axis=0)
    tile_out[...] = jnp.concatenate([both, jnp.zeros((6, LANES), F32)], axis=0)
    high, low = two_parts(both)
    tile = jnp.concatenate([high, low, jnp.zeros((12, LANES), F32)], axis=0).astype(BF16)
    for send in sends.values():
        send[pl.ds(rows, 16), :] = tile


def cast_kernel(t_cur, probes, rounded_probes, *refs):
    *outs, held, sems = refs
    copies = [pltpu.make_async_copy(x, held.at[n], sems.at[n]) for n, x in enumerate((t_cur, probes))]
    for copy in copies:
        copy.start()
    copies[0].wait()
    for out in outs:
        out[...] = held[0].astype(BF16)
    copies[1].wait()
    rounded_probes[...] = held[1].astype(BF16)


def gathered(own, received):
    count, width = own.shape
    total = own[...]
    for r in received:
        total = total + get_halves(r, 0, count, width).astype(F32)
    return total


def next_kernel(n_col, with_probes, own, *refs):
    received, (prev, cur, probes, tile, handed, *outs) = refs[: n_col - 1], refs[n_col - 1 :]
    handed[...] = received[with_probes][pl.ds(own.shape[0] * own.shape[1] // LANES, handed.shape[0]), :]
    value = 2.0 * gathered(own, received) - prev[...]
    for out in outs:
        out[...] = value.astype(BF16)
    ahead = as_row(jnp.sum(probes[...] * value, axis=1, keepdims=True))
    back = as_row(jnp.sum(probes[...] * cur[...], axis=1, keepdims=True))
    tile[...] = jnp.concatenate([ahead, -back, jnp.zeros((6, LANES), F32)], axis=0)


def value_kernel(n_col, own, *refs):
    received, (prev, out) = refs[: n_col - 1], refs[n_col - 1 :]
    out[...] = 2.0 * gathered(own, received) - prev[...]


def tile_kernel(start, n_received, mine, *refs):
    received, outs = refs[:n_received], refs[n_received:]
    total = mine[...]
    for r in received:
        t = r[pl.ds(start, 16), :].astype(F32)
        total = total + jnp.concatenate([t[0:2] + t[2:4], jnp.zeros((6, LANES), F32)], axis=0)
    for out in outs:
        out[...] = total


def last_kernel(n_col, coeffs, own, *refs):
    received = refs[: n_col - 1]
    prev, t_next, accum, t_after, accum_out = refs[n_col - 1 :]
    value = 2.0 * gathered(own, received) - prev[...]
    t_after[...] = value
    accum_out[...] = accum[...] + coeffs[0] * t_next[...] + coeffs[1] * value


def local(n_row, n_col, blocks, block_rows, block_cols, block_count, probes, t_prev, t_cur, accum, coeffs):
    n_slots, bs = blocks.shape[2], blocks.shape[-1]
    count, width = t_cur.shape
    pb = width // bs
    total_rows = width * n_row * n_col
    dense_bytes = n_row * n_col * width * width * 2
    params = pltpu.CompilerParams(vmem_limit_bytes=min(60 * 1024 * 1024, 3 * dense_bytes))
    barrier = lax.optimization_barrier

    def swap(x, axis, k):
        n = n_row if axis == "row" else n_col
        return lax.ppermute(x, axis, [(i, i ^ k) for i in range(n)])

    def call(kernel, out_shape, in_specs, name, **more):
        one = not isinstance(out_shape, list)
        return pl.pallas_call(
            kernel,
            out_shape=out_shape,
            in_specs=in_specs,
            out_specs=VMEM if one else [VMEM] * len(out_shape),
            compiler_params=params,
            name=name,
            **more,
        )

    def in_hbm(x):
        return pltpu.with_memory_space_constraint(x, pltpu.HBM)

    def shape(*dims, dtype=F32):
        return jax.ShapeDtypeStruct(dims, dtype)

    group = 8
    dense = call(
        functools.partial(place_kernel, pb, group),
        shape(n_row, pb, n_col * width, bs, dtype=BF16),
        [SMEM] + [HBM] * 3,
        "place",
        scratch_shapes=[
            pltpu.VMEM((n_slots, bs, bs), BF16),
            pltpu.SMEM(block_rows.shape, jnp.int32),
            pltpu.SMEM(block_cols.shape, jnp.int32),
            pltpu.SemaphoreType.DMA((n_slots // group,)),
            pltpu.SemaphoreType.DMA((2,)),
        ],
    )(block_count, *(in_hbm(x) for x in (block_rows, block_cols, blocks)))

    far = list(range(n_row - 2, 0, -2))
    if n_row == 8:
        far = FAR
    n_out = len(far) + 1
    mine_order = [0] + [k ^ 1 for k in far]
    others_order = [1] + far

    def gather(v, *copies):
        got = [swap(copy, "row", k ^ 1) for copy, k in zip(copies, far)]
        return jnp.stack([v] + got[:-1]), got[-1][None]

    rows = width // LANES * count

    def halves(head, tail, kernel, send_order, carried, extra_rows, tail_shapes, name):
        other = [swap(head, "row", 1), swap(tail, "row", 1)]
        half = call(
            functools.partial(first_half_kernel, pb, mine_order),
            shape(n_col, count, width),
            [VMEM] * 2,
            name + "_a",
        )(jnp.concatenate([head, tail]), dense)
        outs = [shape(count, width)]
        outs += [shape(rows + extra_rows.get(m, 0), LANES, dtype=BF16) for m in send_order] + tail_shapes
        return call(
            functools.partial(kernel, pb, others_order, send_order),
            outs,
            [VMEM] * (3 + len(carried)),
            name + "_b",
        )(jnp.concatenate(other), dense, half, *carried)

    first_order = second_order = list(range(1, n_col))
    if n_col == 4:
        first_order, second_order = ORDER1, ORDER2

    def exchange(sends, order):
        return [swap(send, "col", m) for m, send in zip(order, sends)]

    rounded_probes, *v = call(
        cast_kernel,
        [shape(count, width, dtype=BF16)] * (1 + n_out),
        [HBM] * 2,
        "cast",
        scratch_shapes=[pltpu.VMEM((2, count, width), F32), pltpu.SemaphoreType.DMA((2,))],
    )(in_hbm(t_cur), in_hbm(probes))
    head, tail = gather(*v)
    kept = {0: rounded_probes}
    k = n_col // 2
    while k > 1:
        for m in list(kept):
            kept[m ^ k] = swap(kept[m], "col", k)
        k //= 2
    kept = [kept[m] for m in range(0, n_col, 2)]
    head, tail, dense = barrier((head, tail, dense))
    own, *sends = halves(
        head,
        tail,
        lambda *a: second_half_kernel(*a[:3], len(kept), *a[3:]),
        first_order,
        kept,
        {1: rows * len(kept)},
        [],
        "first",
    )
    received = exchange(sends, first_order)
    tile, handed, *rounded = call(
        functools.partial(next_kernel, n_col, first_order.index(1)),
        [shape(8, LANES), shape(rows * len(kept), LANES, dtype=BF16)]
        + [shape(count, width, dtype=BF16)] * n_out,
        [VMEM] * (n_col + 3),
        "next",
    )(own, *received, t_prev, t_cur, probes)
    t_next = call(
        functools.partial(value_kernel, n_col), shape(count, width), [VMEM] * (n_col + 1), "value"
    )(own, *received, t_prev)

    head, tail = gather(*rounded)
    head, tail, t_next = barrier((head, tail, t_next))
    own, *sends, mine = halves(
        head,
        tail,
        lambda *a: second_half_moment_kernel(*a[:3], len(kept), *a[3:]),
        second_order,
        [tile, handed, probes] + kept[1:],
        dict.fromkeys(second_order, 16),
        [shape(8, LANES)],
        "second",
    )
    received = exchange(sends, second_order)
    total, *tiles = call(
        functools.partial(tile_kernel, rows, n_col - 1), [shape(8, LANES)] * n_out, [VMEM] * n_col, "sums"
    )(mine, *received)
    t_after, accum_out = call(
        functools.partial(last_kernel, n_col),
        [shape(count, width), shape(count, width)],
        [SMEM] + [VMEM] * (n_col + 3),
        "last",
    )(coeffs, own, *received, t_cur, t_next, accum)

    got = [swap(tile, "row", k ^ 1) for tile, k in zip(tiles, far)]
    got, t_after, accum_out = barrier((got, t_after, accum_out))
    for one in got:
        total = total + one
    total = total + swap(total, "row", 1)
    moments = total[:2, :count] * float(total_rows) ** (-0.5)
    return (t_next, t_after, accum_out, moments)


def solution(mesh):
    vector = P(None, ("row", "col"))
    return jax.shard_map(
        functools.partial(local, mesh.shape["row"], mesh.shape["col"]),
        mesh=mesh,
        in_specs=(
            P("row", "col", None, None, None),
            P("row", "col", None),
            P("row", "col", None),
            P("row", "col"),
            vector,
            vector,
            vector,
            vector,
            P(),
        ),
        out_specs=(vector, vector, vector, P()),
        check_vma=False,
    )
```

```python
import functools

import jax
import jax.numpy as jnp
from jax import lax
from jax.experimental import pallas as pl
from jax.experimental.pallas import tpu as pltpu
from jax.sharding import PartitionSpec as P

VMEM = pl.BlockSpec(memory_space=pltpu.VMEM)
SMEM = pl.BlockSpec(memory_space=pltpu.SMEM)
HBM = pl.BlockSpec(memory_space=pltpu.HBM)
CONTRACT_LAST = (((1,), (1,)), ((), ()))
F32, BF16 = jnp.float32, jnp.bfloat16
LANES = 128
ORDER1 = [3, 2, 1]
ORDER2 = [2, 3, 1]
FAR_A, FAR_C, FAR_M = [6, 4, 2], [4, 2, 6], [6, 4, 2]


def place_kernel(pb, group, count, rows_in, cols_in, blocks, dense, held, rows, cols, sems, own_sems):
    r, c = lax.axis_index("row"), lax.axis_index("col")
    bs = blocks.shape[-1]
    groups = held.shape[0] // group

    def fetch(g):
        span = pl.ds(g * group, group)
        return pltpu.make_async_copy(blocks.at[0, 0, span], held.at[span], sems.at[g])

    names = (
        pltpu.make_async_copy(rows_in, rows, own_sems.at[0]),
        pltpu.make_async_copy(cols_in, cols, own_sems.at[1]),
    )
    for copy in names:
        copy.start()
    for g in range(groups):
        fetch(g).start()
    dense[...] = jnp.zeros_like(dense)
    for copy in names:
        copy.wait()
    live = count[0, 0]

    def put(slot):
        @pl.when(slot < live)
        def _():
            i, j = rows[0, 0, slot], cols[0, 0, slot]
            line = ((i // pb) ^ c) * pb + i % pb
            dense[(j // pb) ^ r, j % pb, pl.ds(pl.multiple_of(line * bs, bs), bs), :] = held[slot]

    for g in range(groups):
        fetch(g).wait()
        for n in range(group):
            put(g * group + n)


def dots(pb, order, vectors, dense, m, width):
    total = None
    for h, k in enumerate(order):
        w = jnp.concatenate([dense[k, s, pl.ds(m * width, width), :] for s in range(pb)], axis=1)
        part = lax.dot_general(vectors[h], w, CONTRACT_LAST, preferred_element_type=F32)
        total = part if total is None else total + part
    return total


def start_kernel(pb, order, vectors, dense, out):
    width = vectors.shape[2]
    for m in range(out.shape[0]):
        out[m] = dots(pb, order, vectors, dense, m, width)


def more_kernel(pb, order, vectors, dense, before, out):
    width = vectors.shape[2]
    for m in range(out.shape[0]):
        out[m] = before[m] + dots(pb, order, vectors, dense, m, width)


def as_row(column):
    n = column.shape[0]
    shape = (n, LANES)
    here = lax.broadcasted_iota(jnp.int32, shape, 0) == lax.broadcasted_iota(jnp.int32, shape, 1)
    return jnp.sum(jnp.where(here, column, 0.0), axis=0, keepdims=True)


def two_parts(x):
    high = x.astype(BF16).astype(F32)
    return high, x - high


def put_halves(ref, start, value):
    count = value.shape[0]
    for s in range(value.shape[1] // LANES):
        ref[pl.ds(start + s * count, count), :] = value[:, s * LANES : (s + 1) * LANES]


def get_halves(ref, start, count, width):
    return jnp.concatenate(
        [ref[pl.ds(start + s * count, count), :] for s in range(width // LANES)], axis=1
    )


def end_kernel(pb, order, send_order, vectors, dense, before, own, *refs):
    width, sends = vectors.shape[2], dict(zip(send_order, refs))
    for m in range(before.shape[0]):
        total = before[m] + dots(pb, order, vectors, dense, m, width)
        if m == 0:
            own[...] = total
        else:
            put_halves(sends[m], 0, total.astype(BF16))


def end_moment_kernel(pb, order, send_order, n_kept, vectors, dense, half, before, handed, *refs):
    width, chunks = vectors.shape[2], half.shape[0]
    kept, own, tile_out = refs[:n_kept], refs[n_kept], refs[-1]
    sends = dict(zip(send_order, refs[n_kept + 1 : -1]))
    count = own.shape[0]
    rows = count * width // LANES
    sums = None
    for m in range(chunks):
        total = half[m] + dots(pb, order, vectors, dense, m, width)
        probes = (handed[m - n_kept] if m >= n_kept else kept[m][...]).astype(F32)
        part = jnp.sum(probes * total, axis=1, keepdims=True)
        sums = part if sums is None else sums + part
        if m == 0:
            own[...] = total
        else:
            put_halves(sends[m], 0, total.astype(BF16))
    both = before[...][:2] + jnp.concatenate([jnp.zeros((1, LANES), F32), 2.0 * as_row(sums)], axis=0)
    tile_out[...] = jnp.concatenate([both, jnp.zeros((6, LANES), F32)], axis=0)
    high, low = two_parts(both)
    tile = jnp.concatenate([high, low, jnp.zeros((12, LANES), F32)], axis=0).astype(BF16)
    for send in sends.values():
        send[pl.ds(rows, 16), :] = tile


def cast_kernel(t_cur, probes, rounded_probes, *refs):
    *outs, held, sems = refs
    copies = [pltpu.make_async_copy(x, held.at[n], sems.at[n]) for n, x in enumerate((t_cur, probes))]
    for copy in copies:
        copy.start()
    copies[0].wait()
    for out in outs:
        out[...] = held[0].astype(BF16)
    copies[1].wait()
    rounded_probes[...] = held[1].astype(BF16)


def gathered(own, received):
    count, width = own.shape
    total = own[...]
    for r in received:
        total = total + get_halves(r, 0, count, width).astype(F32)
    return total


def next_kernel(n_col, own, *refs):
    received, (prev, cur, probes, tile, *outs) = refs[: n_col - 1], refs[n_col - 1 :]
    value = 2.0 * gathered(own, received) - prev[...]
    for out in outs:
        out[...] = value.astype(BF16)
    ahead = as_row(jnp.sum(probes[...] * value, axis=1, keepdims=True))
    back = as_row(jnp.sum(probes[...] * cur[...], axis=1, keepdims=True))
    tile[...] = jnp.concatenate([ahead, -back, jnp.zeros((6, LANES), F32)], axis=0)


def value_kernel(n_col, own, *refs):
    received, (prev, out) = refs[: n_col - 1], refs[n_col - 1 :]
    out[...] = 2.0 * gathered(own, received) - prev[...]


def tile_kernel(start, n_received, mine, *refs):
    received, outs = refs[:n_received], refs[n_received:]
    total = mine[...]
    for r in received:
        t = r[pl.ds(start, 16), :].astype(F32)
        total = total + jnp.concatenate([t[0:2] + t[2:4], jnp.zeros((6, LANES), F32)], axis=0)
    for out in outs:
        out[...] = total


def last_kernel(n_col, coeffs, own, *refs):
    received = refs[: n_col - 1]
    prev, t_next, accum, t_after, accum_out = refs[n_col - 1 :]
    value = 2.0 * gathered(own, received) - prev[...]
    t_after[...] = value
    accum_out[...] = accum[...] + coeffs[0] * t_next[...] + coeffs[1] * value


def local(n_row, n_col, blocks, block_rows, block_cols, block_count, probes, t_prev, t_cur, accum, coeffs):
    n_slots, bs = blocks.shape[2], blocks.shape[-1]
    count, width = t_cur.shape
    pb = width // bs
    total_rows = width * n_row * n_col
    dense_bytes = n_row * n_col * width * width * 2
    params = pltpu.CompilerParams(vmem_limit_bytes=min(60 * 1024 * 1024, 3 * dense_bytes))
    barrier = lax.optimization_barrier

    def swap(x, axis, k):
        n = n_row if axis == "row" else n_col
        return lax.ppermute(x, axis, [(i, i ^ k) for i in range(n)])

    def call(kernel, out_shape, in_specs, name, **more):
        one = not isinstance(out_shape, list)
        return pl.pallas_call(
            kernel,
            out_shape=out_shape,
            in_specs=in_specs,
            out_specs=VMEM if one else [VMEM] * len(out_shape),
            compiler_params=params,
            name=name,
            **more,
        )

    def in_hbm(x):
        return pltpu.with_memory_space_constraint(x, pltpu.HBM)

    def shape(*dims, dtype=F32):
        return jax.ShapeDtypeStruct(dims, dtype)

    group = 8
    dense = call(
        functools.partial(place_kernel, pb, group),
        shape(n_row, pb, n_col * width, bs, dtype=BF16),
        [SMEM] + [HBM] * 3,
        "place",
        scratch_shapes=[
            pltpu.VMEM((n_slots, bs, bs), BF16),
            pltpu.SMEM(block_rows.shape, jnp.int32),
            pltpu.SMEM(block_cols.shape, jnp.int32),
            pltpu.SemaphoreType.DMA((n_slots // group,)),
            pltpu.SemaphoreType.DMA((2,)),
        ],
    )(block_count, *(in_hbm(x) for x in (block_rows, block_cols, blocks)))

    far = list(range(n_row - 2, 0, -2))
    orders = [FAR_A, FAR_C, FAR_M] if n_row == 8 else [far] * 3
    n_out = len(far) + 1
    def gather(far, v, *copies):
        got = [swap(copy, "row", k ^ 1) for copy, k in zip(copies, far)]
        return jnp.stack([v] + got[:-1]), got[-1][None]

    rows = width // LANES * count

    def multiply(early, far, head, tail, kernel, send_order, carried, extra_rows, tail_shapes, name):
        mine_order, others_order = [0] + [k ^ 1 for k in far], [1] + far
        other_head, other_tail = swap(head, "row", 1), swap(tail, "row", 1)
        sums = shape(n_col, count, width)
        most = call(
            functools.partial(start_kernel, pb, mine_order), sums, [VMEM] * 2, name + "_start"
        )(jnp.concatenate([head, tail]), dense)
        last_order, others = others_order, jnp.concatenate([other_head, other_tail])
        if early:
            most = call(
                functools.partial(more_kernel, pb, others_order[:-1]), sums, [VMEM] * 3, name + "_more"
            )(other_head, dense, most)
            last_order, others = others_order[-1:], other_tail
        outs = [shape(count, width)]
        outs += [shape(rows + extra_rows.get(m, 0), LANES, dtype=BF16) for m in send_order] + tail_shapes
        return call(
            functools.partial(kernel, pb, last_order, send_order),
            outs,
            [VMEM] * (3 + len(carried)),
            name + "_end",
        )(others, dense, most, *carried)

    first_order = second_order = list(range(1, n_col))
    if n_col == 4:
        first_order, second_order = ORDER1, ORDER2

    def exchange(sends, order):
        return [swap(send, "col", m) for m, send in zip(order, sends)]

    rounded_probes, *v = call(
        cast_kernel,
        [shape(count, width, dtype=BF16)] * (1 + n_out),
        [HBM] * 2,
        "cast",
        scratch_shapes=[pltpu.VMEM((2, count, width), F32), pltpu.SemaphoreType.DMA((2,))],
    )(in_hbm(t_cur), in_hbm(probes))
    head, tail = gather(orders[0], *v)
    kept, k = [rounded_probes], 1
    while 2 * k < n_col:
        kept += [swap(piece, "col", k) for piece in kept]
        k *= 2
    tail, dense = barrier((tail, dense))
    own, *sends = multiply(
        True,
        orders[0],
        head,
        tail,
        end_kernel,
        first_order,
        [],
        {},
        [],
        "first",
    )
    sends, kept = barrier((sends, kept))
    handed = swap(jnp.stack(kept), "col", k)
    received = exchange(sends, first_order)
    tile, *rounded = call(
        functools.partial(next_kernel, n_col),
        [shape(8, LANES)] + [shape(count, width, dtype=BF16)] * n_out,
        [VMEM] * (n_col + 3),
        "next",
    )(own, *received, t_prev, t_cur, probes)
    t_next = call(
        functools.partial(value_kernel, n_col), shape(count, width), [VMEM] * (n_col + 1), "value"
    )(own, *received, t_prev)

    head, tail = gather(orders[1], *rounded)
    tail, t_next, handed = barrier((tail, t_next, handed))
    own, *sends, mine = multiply(
        False,
        orders[1],
        head,
        tail,
        lambda *a: end_moment_kernel(*a[:3], len(kept), *a[3:]),
        second_order,
        [tile, handed, probes] + kept[1:],
        dict.fromkeys(second_order, 16),
        [shape(8, LANES)],
        "second",
    )
    received = exchange(sends, second_order)
    total, *tiles = call(
        functools.partial(tile_kernel, rows, n_col - 1), [shape(8, LANES)] * n_out, [VMEM] * n_col, "sums"
    )(mine, *received)
    t_after, accum_out = call(
        functools.partial(last_kernel, n_col),
        [shape(count, width), shape(count, width)],
        [SMEM] + [VMEM] * (n_col + 3),
        "last",
    )(coeffs, own, *received, t_cur, t_next, accum)

    got = [swap(tile, "row", k ^ 1) for tile, k in zip(tiles, orders[2])]
    got, t_after, accum_out = barrier((got, t_after, accum_out))
    for one in got:
        total = total + one
    total = total + swap(total, "row", 1)
    moments = total[:2, :count] * float(total_rows) ** (-0.5)
    return (t_next, t_after, accum_out, moments)


def solution(mesh):
    vector = P(None, ("row", "col"))
    return jax.shard_map(
        functools.partial(local, mesh.shape["row"], mesh.shape["col"]),
        mesh=mesh,
        in_specs=(
            P("row", "col", None, None, None),
            P("row", "col", None),
            P("row", "col", None),
            P("row", "col"),
            vector,
            vector,
            vector,
            vector,
            P(),
        ),
        out_specs=(vector, vector, vector, P()),
        check_vma=False,
    )
```

```python
import functools

import jax
import jax.numpy as jnp
from jax import lax
from jax.experimental import pallas as pl
from jax.experimental.pallas import tpu as pltpu
from jax.sharding import PartitionSpec as P

VMEM = pl.BlockSpec(memory_space=pltpu.VMEM)
SMEM = pl.BlockSpec(memory_space=pltpu.SMEM)
HBM = pl.BlockSpec(memory_space=pltpu.HBM)
CONTRACT_LAST = (((1,), (1,)), ((), ()))
F32, BF16 = jnp.float32, jnp.bfloat16
LANES = 128
ORDER1 = [3, 2, 1]
ORDER2 = [2, 3, 1]
FAR_A, FAR_C, FAR_M = [6, 4, 2], [6, 4, 2], [6, 4, 2]


def place_kernel(pb, group, count, rows_in, cols_in, blocks, dense, held, rows, cols, sems, own_sems):
    r, c = lax.axis_index("row"), lax.axis_index("col")
    bs = blocks.shape[-1]
    groups = held.shape[0] // group

    def fetch(g):
        span = pl.ds(g * group, group)
        return pltpu.make_async_copy(blocks.at[0, 0, span], held.at[span], sems.at[g])

    names = (
        pltpu.make_async_copy(rows_in, rows, own_sems.at[0]),
        pltpu.make_async_copy(cols_in, cols, own_sems.at[1]),
    )
    for copy in names:
        copy.start()
    for g in range(groups):
        fetch(g).start()
    dense[...] = jnp.zeros_like(dense)
    for copy in names:
        copy.wait()
    live = count[0, 0]

    def put(slot):
        @pl.when(slot < live)
        def _():
            column, line = cols[0, 0, slot] ^ (r * pb), rows[0, 0, slot] ^ (c * pb)
            dense[column, pl.ds(pl.multiple_of(line * bs, bs), bs), :] = held[slot]

    for g in range(groups):
        fetch(g).wait()
        for n in range(group):
            put(g * group + n)


def dots(pb, order, vectors, dense, m, width):
    total = None
    for h, k in enumerate(order):
        w = jnp.concatenate([dense[k * pb + s, pl.ds(m * width, width), :] for s in range(pb)], axis=1)
        part = lax.dot_general(vectors[h], w, CONTRACT_LAST, preferred_element_type=F32)
        total = part if total is None else total + part
    return total


def start_kernel(pb, order, vectors, dense, out):
    width = vectors.shape[2]
    for m in range(out.shape[0]):
        out[m] = dots(pb, order, vectors, dense, m, width)


def more_kernel(pb, order, vectors, dense, before, out):
    width = vectors.shape[2]
    for m in range(out.shape[0]):
        out[m] = before[m] + dots(pb, order, vectors, dense, m, width)


def as_row(column):
    n = column.shape[0]
    shape = (n, LANES)
    here = lax.broadcasted_iota(jnp.int32, shape, 0) == lax.broadcasted_iota(jnp.int32, shape, 1)
    return jnp.sum(jnp.where(here, column, 0.0), axis=0, keepdims=True)


def two_parts(x):
    high = x.astype(BF16).astype(F32)
    return high, x - high


def put_halves(ref, start, value):
    count = value.shape[0]
    for s in range(value.shape[1] // LANES):
        ref[pl.ds(start + s * count, count), :] = value[:, s * LANES : (s + 1) * LANES]


def get_halves(ref, start, count, width):
    return jnp.concatenate(
        [ref[pl.ds(start + s * count, count), :] for s in range(width // LANES)], axis=1
    )


def end_kernel(pb, order, send_order, vectors, dense, before, own, *refs):
    width, sends = vectors.shape[2], dict(zip(send_order, refs))
    for m in range(before.shape[0]):
        total = before[m] + dots(pb, order, vectors, dense, m, width)
        if m == 0:
            own[...] = total
        else:
            put_halves(sends[m], 0, total.astype(BF16))


def end_moment_kernel(pb, order, send_order, n_kept, vectors, dense, half, before, handed, *refs):
    width, chunks = vectors.shape[2], half.shape[0]
    kept, own, tile_out = refs[:n_kept], refs[n_kept], refs[-1]
    sends = dict(zip(send_order, refs[n_kept + 1 : -1]))
    count = own.shape[0]
    rows = count * width // LANES
    sums = None
    for m in range(chunks):
        total = half[m] + dots(pb, order, vectors, dense, m, width)
        probes = (handed[m - n_kept] if m >= n_kept else kept[m][...]).astype(F32)
        part = jnp.sum(probes * total, axis=1, keepdims=True)
        sums = part if sums is None else sums + part
        if m == 0:
            own[...] = total
        else:
            put_halves(sends[m], 0, total.astype(BF16))
    both = before[...][:2] + jnp.concatenate([jnp.zeros((1, LANES), F32), 2.0 * as_row(sums)], axis=0)
    tile_out[...] = jnp.concatenate([both, jnp.zeros((6, LANES), F32)], axis=0)
    high, low = two_parts(both)
    tile = jnp.concatenate([high, low, jnp.zeros((12, LANES), F32)], axis=0).astype(BF16)
    for send in sends.values():
        send[pl.ds(rows, 16), :] = tile


def cast_kernel(t_cur, probes, rounded_probes, *refs):
    *outs, held, sems = refs
    copies = [pltpu.make_async_copy(x, held.at[n], sems.at[n]) for n, x in enumerate((t_cur, probes))]
    for copy in copies:
        copy.start()
    copies[0].wait()
    for out in outs:
        out[...] = held[0].astype(BF16)
    copies[1].wait()
    rounded_probes[...] = held[1].astype(BF16)


def gathered(own, received):
    count, width = own.shape
    total = own[...]
    for r in received:
        total = total + get_halves(r, 0, count, width).astype(F32)
    return total


def next_kernel(n_col, own, *refs):
    received, (prev, cur, probes, tile, *outs) = refs[: n_col - 1], refs[n_col - 1 :]
    value = 2.0 * gathered(own, received) - prev[...]
    for out in outs:
        out[...] = value.astype(BF16)
    ahead = as_row(jnp.sum(probes[...] * value, axis=1, keepdims=True))
    back = as_row(jnp.sum(probes[...] * cur[...], axis=1, keepdims=True))
    tile[...] = jnp.concatenate([ahead, -back, jnp.zeros((6, LANES), F32)], axis=0)


def value_kernel(n_col, own, *refs):
    received, (prev, out) = refs[: n_col - 1], refs[n_col - 1 :]
    out[...] = 2.0 * gathered(own, received) - prev[...]


def tile_kernel(start, n_received, mine, *refs):
    received, outs = refs[:n_received], refs[n_received:]
    total = mine[...]
    for r in received:
        t = r[pl.ds(start, 16), :].astype(F32)
        total = total + jnp.concatenate([t[0:2] + t[2:4], jnp.zeros((6, LANES), F32)], axis=0)
    for out in outs:
        out[...] = total


def last_kernel(n_col, coeffs, own, *refs):
    received = refs[: n_col - 1]
    prev, t_next, accum, t_after, accum_out = refs[n_col - 1 :]
    value = 2.0 * gathered(own, received) - prev[...]
    t_after[...] = value
    accum_out[...] = accum[...] + coeffs[0] * t_next[...] + coeffs[1] * value


def local(n_row, n_col, blocks, block_rows, block_cols, block_count, probes, t_prev, t_cur, accum, coeffs):
    n_slots, bs = blocks.shape[2], blocks.shape[-1]
    count, width = t_cur.shape
    pb = width // bs
    total_rows = width * n_row * n_col
    dense_bytes = n_row * n_col * width * width * 2
    params = pltpu.CompilerParams(vmem_limit_bytes=min(60 * 1024 * 1024, 3 * dense_bytes))
    barrier = lax.optimization_barrier

    def swap(x, axis, k):
        n = n_row if axis == "row" else n_col
        return lax.ppermute(x, axis, [(i, i ^ k) for i in range(n)])

    def call(kernel, out_shape, in_specs, name, **more):
        one = not isinstance(out_shape, list)
        return pl.pallas_call(
            kernel,
            out_shape=out_shape,
            in_specs=in_specs,
            out_specs=VMEM if one else [VMEM] * len(out_shape),
            compiler_params=params,
            name=name,
            **more,
        )

    def in_hbm(x):
        return pltpu.with_memory_space_constraint(x, pltpu.HBM)

    def shape(*dims, dtype=F32):
        return jax.ShapeDtypeStruct(dims, dtype)

    group = 8
    dense = call(
        functools.partial(place_kernel, pb, group),
        shape(n_row * pb, n_col * width, bs, dtype=BF16),
        [SMEM] + [HBM] * 3,
        "place",
        scratch_shapes=[
            pltpu.VMEM((n_slots, bs, bs), BF16),
            pltpu.SMEM(block_rows.shape, jnp.int32),
            pltpu.SMEM(block_cols.shape, jnp.int32),
            pltpu.SemaphoreType.DMA((n_slots // group,)),
            pltpu.SemaphoreType.DMA((2,)),
        ],
    )(block_count, *(in_hbm(x) for x in (block_rows, block_cols, blocks)))

    far = list(range(n_row - 2, 0, -2))
    orders = [FAR_A, FAR_C, FAR_M] if n_row == 8 else [far] * 3
    n_out = len(far) + 1
    def gather(far, v, *copies):
        return [v] + [swap(copy, "row", k ^ 1) for copy, k in zip(copies, far)]

    rows = width // LANES * count

    def multiply(split, early, late, order, kernel, send_order, carried, extra_rows, tail_shapes, name):
        other_early, other_late = swap(early, "row", 1), swap(late, "row", 1)
        sums, others_order = shape(n_col, count, width), [k ^ 1 for k in order]
        n_early = early.shape[0]
        first, second = (early, jnp.concatenate([late, other_early])) if split else (jnp.concatenate([early, late]), other_early)
        n_first = first.shape[0]
        both = order + others_order
        most = call(
            functools.partial(start_kernel, pb, both[:n_first]), sums, [VMEM] * 2, name + "_start"
        )(first, dense)
        most = call(
            functools.partial(more_kernel, pb, both[n_first : len(order) + n_early]),
            sums,
            [VMEM] * 3,
            name + "_more",
        )(second, dense, most)
        outs = [shape(count, width)]
        outs += [shape(rows + extra_rows.get(m, 0), LANES, dtype=BF16) for m in send_order] + tail_shapes
        return call(
            functools.partial(kernel, pb, others_order[n_early:], send_order),
            outs,
            [VMEM] * (3 + len(carried)),
            name + "_end",
        )(other_late, dense, most, *carried)

    first_order = second_order = list(range(1, n_col))
    if n_col == 4:
        first_order, second_order = ORDER1, ORDER2

    def exchange(sends, order):
        return [swap(send, "col", m) for m, send in zip(order, sends)]

    rounded_probes, *v = call(
        cast_kernel,
        [shape(count, width, dtype=BF16)] * (1 + n_out),
        [HBM] * 2,
        "cast",
        scratch_shapes=[pltpu.VMEM((2, count, width), F32), pltpu.SemaphoreType.DMA((2,))],
    )(in_hbm(t_cur), in_hbm(probes))
    got = gather(orders[0], *v)
    kept, k = [rounded_probes], 1
    while 2 * k < n_col:
        kept += [swap(piece, "col", k) for piece in kept]
        k *= 2
    got[-1], dense = barrier((got[-1], dense))
    own, *sends = multiply(
        False,
        jnp.stack(got[:-1]),
        got[-1][None],
        [0] + [k ^ 1 for k in orders[0]],
        end_kernel,
        first_order,
        [],
        {},
        [],
        "first",
    )
    sends, kept = barrier((sends, kept))
    handed = swap(jnp.stack(kept), "col", k)
    received = exchange(sends, first_order)
    tile, *rounded = call(
        functools.partial(next_kernel, n_col),
        [shape(8, LANES)] + [shape(count, width, dtype=BF16)] * n_out,
        [VMEM] * (n_col + 3),
        "next",
    )(own, *received, t_prev, t_cur, probes)
    t_next = call(
        functools.partial(value_kernel, n_col), shape(count, width), [VMEM] * (n_col + 1), "value"
    )(own, *received, t_prev)

    got = gather(orders[1], *rounded)
    got[1], t_next, handed = barrier((got[1], t_next, handed))
    own, *sends, mine = multiply(
        True,
        jnp.stack(got[:2]),
        jnp.stack(got[2:]),
        [0] + [k ^ 1 for k in orders[1]],
        lambda *a: end_moment_kernel(*a[:3], len(kept), *a[3:]),
        second_order,
        [tile, handed, probes] + kept[1:],
        dict.fromkeys(second_order, 16),
        [shape(8, LANES)],
        "second",
    )
    received = exchange(sends, second_order)
    total, *tiles = call(
        functools.partial(tile_kernel, rows, n_col - 1), [shape(8, LANES)] * n_out, [VMEM] * n_col, "sums"
    )(mine, *received)
    t_after, accum_out = call(
        functools.partial(last_kernel, n_col),
        [shape(count, width), shape(count, width)],
        [SMEM] + [VMEM] * (n_col + 3),
        "last",
    )(coeffs, own, *received, t_cur, t_next, accum)

    got = [swap(tile, "row", k ^ 1) for tile, k in zip(tiles, orders[2])]
    got, t_after, accum_out = barrier((got, t_after, accum_out))
    for one in got:
        total = total + one
    total = total + swap(total, "row", 1)
    moments = total[:2, :count] * float(total_rows) ** (-0.5)
    return (t_next, t_after, accum_out, moments)


def solution(mesh):
    vector = P(None, ("row", "col"))
    return jax.shard_map(
        functools.partial(local, mesh.shape["row"], mesh.shape["col"]),
        mesh=mesh,
        in_specs=(
            P("row", "col", None, None, None),
            P("row", "col", None),
            P("row", "col", None),
            P("row", "col"),
            vector,
            vector,
            vector,
            vector,
            P(),
        ),
        out_specs=(vector, vector, vector, P()),
        check_vma=False,
    )
```

```python
import functools

import jax
import jax.numpy as jnp
from jax import lax
from jax.experimental import pallas as pl
from jax.experimental.pallas import tpu as pltpu
from jax.sharding import PartitionSpec as P

VMEM = pl.BlockSpec(memory_space=pltpu.VMEM)
SMEM = pl.BlockSpec(memory_space=pltpu.SMEM)
HBM = pl.BlockSpec(memory_space=pltpu.HBM)
CONTRACT_LAST = (((1,), (1,)), ((), ()))
F32, BF16, F16 = jnp.float32, jnp.bfloat16, jnp.float16
SCALE, TILE_SCALE = 2.0**-6, 2.0**-16
LANES = 128
ORDER1 = [1, 2, 3]
ORDER2 = [2, 1, 3]
FAR_A, FAR_C, FAR_M = [6, 4, 2], [6, 4, 2], [6, 4, 2]


def place_kernel(pb, group, count, rows_in, cols_in, blocks, dense, held, rows, cols, sems, own_sems):
    r, c = lax.axis_index("row"), lax.axis_index("col")
    bs = blocks.shape[-1]
    groups = held.shape[0] // group

    def fetch(g):
        span = pl.ds(g * group, group)
        return pltpu.make_async_copy(blocks.at[0, 0, span], held.at[span], sems.at[g])

    names = (
        pltpu.make_async_copy(rows_in, rows, own_sems.at[0]),
        pltpu.make_async_copy(cols_in, cols, own_sems.at[1]),
    )
    for copy in names:
        copy.start()
    for g in range(groups):
        fetch(g).start()
    dense[...] = jnp.zeros_like(dense)
    for copy in names:
        copy.wait()
    live = count[0, 0]

    def put(slot):
        @pl.when(slot < live)
        def _():
            column, line = cols[0, 0, slot] ^ (r * pb), rows[0, 0, slot] ^ (c * pb)
            dense[column, pl.ds(pl.multiple_of(line * bs, bs), bs), :] = held[slot]

    for g in range(groups):
        fetch(g).wait()
        for n in range(group):
            put(g * group + n)


def dots(pb, order, vectors, dense, m, width):
    total = None
    for h, k in enumerate(order):
        w = jnp.concatenate([dense[k * pb + s, pl.ds(m * width, width), :] for s in range(pb)], axis=1)
        part = lax.dot_general(vectors[h], w, CONTRACT_LAST, preferred_element_type=F32)
        total = part if total is None else total + part
    return total


def start_kernel(pb, order, vectors, dense, out):
    width = vectors.shape[2]
    for m in range(out.shape[0]):
        out[m] = dots(pb, order, vectors, dense, m, width)


def more_kernel(pb, order, vectors, dense, before, out):
    width = vectors.shape[2]
    for m in range(out.shape[0]):
        out[m] = before[m] + dots(pb, order, vectors, dense, m, width)


def as_row(column):
    n = column.shape[0]
    shape = (n, LANES)
    here = lax.broadcasted_iota(jnp.int32, shape, 0) == lax.broadcasted_iota(jnp.int32, shape, 1)
    return jnp.sum(jnp.where(here, column, 0.0), axis=0, keepdims=True)


def two_parts(x):
    high = x.astype(BF16).astype(F32)
    return high, x - high


def put_halves(ref, start, value):
    count = value.shape[0]
    for s in range(value.shape[1] // LANES):
        ref[pl.ds(start + s * count, count), :] = value[:, s * LANES : (s + 1) * LANES]


def get_halves(ref, start, count, width):
    return jnp.concatenate(
        [ref[pl.ds(start + s * count, count), :] for s in range(width // LANES)], axis=1
    )


def end_kernel(pb, order, send_order, vectors, dense, before, own, *refs):
    width, sends = vectors.shape[2], dict(zip(send_order, refs))
    for m in range(before.shape[0]):
        total = before[m] + dots(pb, order, vectors, dense, m, width)
        if m == 0:
            own[...] = total
        else:
            put_halves(sends[m], 0, total * SCALE)


def end_moment_kernel(pb, order, send_order, n_kept, vectors, dense, half, before, handed, *refs):
    width, chunks = vectors.shape[2], half.shape[0]
    kept, own, tile_out = refs[:n_kept], refs[n_kept], refs[-1]
    sends = dict(zip(send_order, refs[n_kept + 1 : -1]))
    count = own.shape[0]
    rows = count * width // LANES
    sums = None
    for m in range(chunks):
        total = half[m] + dots(pb, order, vectors, dense, m, width)
        probes = (handed[m - n_kept] if m >= n_kept else kept[m][...]).astype(F32)
        part = jnp.sum(probes * total, axis=1, keepdims=True)
        sums = part if sums is None else sums + part
        if m == 0:
            own[...] = total
        else:
            put_halves(sends[m], 0, total * SCALE)
    both = before[...][:2] + jnp.concatenate([jnp.zeros((1, LANES), F32), 2.0 * as_row(sums)], axis=0)
    tile_out[...] = jnp.concatenate([both, jnp.zeros((6, LANES), F32)], axis=0)
    high, low = two_parts(both * TILE_SCALE)
    tile = jnp.concatenate([high, low, jnp.zeros((12, LANES), F32)], axis=0)
    for send in sends.values():
        send[pl.ds(rows, 16), :] = tile


def cast_kernel(t_cur, probes, rounded_probes, *refs):
    *outs, held, sems = refs
    copies = [pltpu.make_async_copy(x, held.at[n], sems.at[n]) for n, x in enumerate((t_cur, probes))]
    for copy in copies:
        copy.start()
    copies[0].wait()
    for out in outs:
        out[...] = held[0].astype(BF16)
    copies[1].wait()
    rounded_probes[...] = held[1].astype(BF16)


def gathered(own, received):
    count, width = own.shape
    total = own[...]
    for r in received:
        total = total + get_halves(r, 0, count, width) * (1 / SCALE)
    return total


def next_kernel(n_col, own, *refs):
    received, (prev, cur, probes, tile, *outs) = refs[: n_col - 1], refs[n_col - 1 :]
    value = 2.0 * gathered(own, received) - prev[...]
    for out in outs:
        out[...] = value.astype(BF16)
    ahead = as_row(jnp.sum(probes[...] * value, axis=1, keepdims=True))
    back = as_row(jnp.sum(probes[...] * cur[...], axis=1, keepdims=True))
    tile[...] = jnp.concatenate([ahead, -back, jnp.zeros((6, LANES), F32)], axis=0)


def value_kernel(n_col, own, *refs):
    received, (prev, out) = refs[: n_col - 1], refs[n_col - 1 :]
    out[...] = 2.0 * gathered(own, received) - prev[...]


def tile_kernel(start, n_received, mine, *refs):
    received, outs = refs[:n_received], refs[n_received:]
    total = mine[...]
    for r in received:
        t = r[pl.ds(start, 16), :] * (1 / TILE_SCALE)
        total = total + jnp.concatenate([t[0:2] + t[2:4], jnp.zeros((6, LANES), F32)], axis=0)
    for out in outs:
        out[...] = total


def last_kernel(n_col, coeffs, own, *refs):
    received = refs[: n_col - 1]
    prev, t_next, accum, t_after, accum_out = refs[n_col - 1 :]
    value = 2.0 * gathered(own, received) - prev[...]
    t_after[...] = value
    accum_out[...] = accum[...] + coeffs[0] * t_next[...] + coeffs[1] * value


def local(n_row, n_col, blocks, block_rows, block_cols, block_count, probes, t_prev, t_cur, accum, coeffs):
    n_slots, bs = blocks.shape[2], blocks.shape[-1]
    count, width = t_cur.shape
    pb = width // bs
    total_rows = width * n_row * n_col
    dense_bytes = n_row * n_col * width * width * 2
    params = pltpu.CompilerParams(vmem_limit_bytes=min(60 * 1024 * 1024, 3 * dense_bytes))
    barrier = lax.optimization_barrier

    def swap(x, axis, k):
        n = n_row if axis == "row" else n_col
        return lax.ppermute(x, axis, [(i, i ^ k) for i in range(n)])

    def call(kernel, out_shape, in_specs, name, **more):
        one = not isinstance(out_shape, list)
        return pl.pallas_call(
            kernel,
            out_shape=out_shape,
            in_specs=in_specs,
            out_specs=VMEM if one else [VMEM] * len(out_shape),
            compiler_params=params,
            name=name,
            **more,
        )

    def in_hbm(x):
        return pltpu.with_memory_space_constraint(x, pltpu.HBM)

    def shape(*dims, dtype=F32):
        return jax.ShapeDtypeStruct(dims, dtype)

    group = 8
    dense = call(
        functools.partial(place_kernel, pb, group),
        shape(n_row * pb, n_col * width, bs, dtype=BF16),
        [SMEM] + [HBM] * 3,
        "place",
        scratch_shapes=[
            pltpu.VMEM((n_slots, bs, bs), BF16),
            pltpu.SMEM(block_rows.shape, jnp.int32),
            pltpu.SMEM(block_cols.shape, jnp.int32),
            pltpu.SemaphoreType.DMA((n_slots // group,)),
            pltpu.SemaphoreType.DMA((2,)),
        ],
    )(block_count, *(in_hbm(x) for x in (block_rows, block_cols, blocks)))

    far = list(range(n_row - 2, 0, -2))
    orders = [FAR_A, FAR_C, FAR_M] if n_row == 8 else [far] * 3
    n_out = len(far) + 1
    def gather(far, v, *copies):
        return [v] + [swap(copy, "row", k ^ 1) for copy, k in zip(copies, far)]

    rows = width // LANES * count

    def multiply(split, early, late, order, kernel, send_order, carried, extra_rows, tail_shapes, name):
        other_early, other_late = swap(early, "row", 1), swap(late, "row", 1)
        sums, others_order = shape(n_col, count, width), [k ^ 1 for k in order]
        n_early = early.shape[0]
        first, second = (early, jnp.concatenate([late, other_early])) if split else (jnp.concatenate([early, late]), other_early)
        n_first = first.shape[0]
        both = order + others_order
        most = call(
            functools.partial(start_kernel, pb, both[:n_first]), sums, [VMEM] * 2, name + "_start"
        )(first, dense)
        most = call(
            functools.partial(more_kernel, pb, both[n_first : len(order) + n_early]),
            sums,
            [VMEM] * 3,
            name + "_more",
        )(second, dense, most)
        outs = [shape(count, width)]
        outs += [shape(rows + extra_rows.get(m, 0), LANES) for m in send_order] + tail_shapes
        return call(
            functools.partial(kernel, pb, others_order[n_early:], send_order),
            outs,
            [VMEM] * (3 + len(carried)),
            name + "_end",
        )(other_late, dense, most, *carried)

    first_order = second_order = list(range(1, n_col))
    if n_col == 4:
        first_order, second_order = ORDER1, ORDER2

    def exchange(sends, order):
        return [swap(send.astype(F16), "col", m).astype(F32) for m, send in zip(order, sends)]

    rounded_probes, *v = call(
        cast_kernel,
        [shape(count, width, dtype=BF16)] * (1 + n_out),
        [HBM] * 2,
        "cast",
        scratch_shapes=[pltpu.VMEM((2, count, width), F32), pltpu.SemaphoreType.DMA((2,))],
    )(in_hbm(t_cur), in_hbm(probes))
    got = gather(orders[0], *v)
    kept, k = [rounded_probes], 1
    while 2 * k < n_col:
        kept += [swap(piece, "col", k) for piece in kept]
        k *= 2
    got[-1], dense = barrier((got[-1], dense))
    own, *sends = multiply(
        False,
        jnp.stack(got[:-1]),
        got[-1][None],
        [0] + [k ^ 1 for k in orders[0]],
        end_kernel,
        first_order,
        [],
        {},
        [],
        "first",
    )
    sends, kept = barrier((sends, kept))
    handed = swap(jnp.stack(kept), "col", k)
    received = exchange(sends, first_order)
    tile, *rounded = call(
        functools.partial(next_kernel, n_col),
        [shape(8, LANES)] + [shape(count, width, dtype=BF16)] * n_out,
        [VMEM] * (n_col + 3),
        "next",
    )(own, *received, t_prev, t_cur, probes)
    t_next = call(
        functools.partial(value_kernel, n_col), shape(count, width), [VMEM] * (n_col + 1), "value"
    )(own, *received, t_prev)

    got = gather(orders[1], *rounded)
    got[1], t_next, handed = barrier((got[1], t_next, handed))
    own, *sends, mine = multiply(
        True,
        jnp.stack(got[:2]),
        jnp.stack(got[2:]),
        [0] + [k ^ 1 for k in orders[1]],
        lambda *a: end_moment_kernel(*a[:3], len(kept), *a[3:]),
        second_order,
        [tile, handed, probes] + kept[1:],
        dict.fromkeys(second_order, 16),
        [shape(8, LANES)],
        "second",
    )
    received = exchange(sends, second_order)
    total, *tiles = call(
        functools.partial(tile_kernel, rows, n_col - 1), [shape(8, LANES)] * n_out, [VMEM] * n_col, "sums"
    )(mine, *received)
    t_after, accum_out = call(
        functools.partial(last_kernel, n_col),
        [shape(count, width), shape(count, width)],
        [SMEM] + [VMEM] * (n_col + 3),
        "last",
    )(coeffs, own, *received, t_cur, t_next, accum)

    got = [swap(tile, "row", k ^ 1) for tile, k in zip(tiles, orders[2])]
    got, t_after, accum_out = barrier((got, t_after, accum_out))
    for one in got:
        total = total + one
    scale = float(total_rows) ** (-0.5)
    other = swap(total, "row", 1)
    moments = (total[:2, :count] + other[:2, :count]) * scale
    return (t_next, t_after, accum_out, moments)


def solution(mesh):
    vector = P(None, ("row", "col"))
    return jax.shard_map(
        functools.partial(local, mesh.shape["row"], mesh.shape["col"]),
        mesh=mesh,
        in_specs=(
            P("row", "col", None, None, None),
            P("row", "col", None),
            P("row", "col", None),
            P("row", "col"),
            vector,
            vector,
            vector,
            vector,
            P(),
        ),
        out_specs=(vector, vector, vector, P()),
        check_vma=False,
    )
```

```python
import functools

import jax
import jax.numpy as jnp
from jax import lax
from jax.experimental import pallas as pl
from jax.experimental.pallas import tpu as pltpu
from jax.sharding import PartitionSpec as P

VMEM = pl.BlockSpec(memory_space=pltpu.VMEM)
SMEM = pl.BlockSpec(memory_space=pltpu.SMEM)
HBM = pl.BlockSpec(memory_space=pltpu.HBM)
CONTRACT_LAST = (((1,), (1,)), ((), ()))
F32, BF16 = jnp.float32, jnp.bfloat16
LANES = 128
ORDER1 = [3, 2, 1]
ORDER2 = [3, 1, 2]
FAR_A, FAR_C, FAR_M = [6, 4, 2], [6, 4, 2], [6, 4, 2]


def place_kernel(pb, group, count, rows_in, cols_in, blocks, dense, held, rows, cols, sems, own_sems):
    r, c = lax.axis_index("row"), lax.axis_index("col")
    bs = blocks.shape[-1]
    groups = held.shape[0] // group

    def fetch(g):
        span = pl.ds(g * group, group)
        return pltpu.make_async_copy(blocks.at[0, 0, span], held.at[span], sems.at[g])

    names = (
        pltpu.make_async_copy(rows_in, rows, own_sems.at[0]),
        pltpu.make_async_copy(cols_in, cols, own_sems.at[1]),
    )
    for copy in names:
        copy.start()
    for g in range(groups):
        fetch(g).start()
    dense[...] = jnp.zeros_like(dense)
    for copy in names:
        copy.wait()
    live = count[0, 0]

    def put(slot):
        @pl.when(slot < live)
        def _():
            column, line = cols[0, 0, slot] ^ (r * pb), rows[0, 0, slot] ^ (c * pb)
            dense[column, pl.ds(pl.multiple_of(line * bs, bs), bs), :] = held[slot]

    for g in range(groups):
        fetch(g).wait()
        for n in range(group):
            put(g * group + n)


def dots(pb, order, vectors, dense, m, width):
    total = None
    for h, k in enumerate(order):
        w = jnp.concatenate([dense[k * pb + s, pl.ds(m * width, width), :] for s in range(pb)], axis=1)
        part = lax.dot_general(vectors[h], w, CONTRACT_LAST, preferred_element_type=F32)
        total = part if total is None else total + part
    return total


def start_kernel(pb, order, vectors, dense, out):
    width = vectors.shape[2]
    for m in range(out.shape[0]):
        out[m] = dots(pb, order, vectors, dense, m, width)


def more_kernel(pb, order, vectors, dense, before, out):
    width = vectors.shape[2]
    for m in range(out.shape[0]):
        out[m] = before[m] + dots(pb, order, vectors, dense, m, width)


def as_row(column):
    n = column.shape[0]
    shape = (n, LANES)
    here = lax.broadcasted_iota(jnp.int32, shape, 0) == lax.broadcasted_iota(jnp.int32, shape, 1)
    return jnp.sum(jnp.where(here, column, 0.0), axis=0, keepdims=True)


def two_parts(x):
    high = x.astype(BF16).astype(F32)
    return high, x - high


def put_halves(ref, start, value):
    count = value.shape[0]
    for s in range(value.shape[1] // LANES):
        ref[pl.ds(start + s * count, count), :] = value[:, s * LANES : (s + 1) * LANES]


def get_halves(ref, start, count, width):
    return jnp.concatenate(
        [ref[pl.ds(start + s * count, count), :] for s in range(width // LANES)], axis=1
    )


def end_kernel(pb, order, send_order, vectors, dense, before, own, *refs):
    width, sends = vectors.shape[2], dict(zip(send_order, refs))
    for m in range(before.shape[0]):
        total = before[m] + dots(pb, order, vectors, dense, m, width)
        if m == 0:
            own[...] = total
        else:
            put_halves(sends[m], 0, total.astype(BF16))


def end_moment_kernel(pb, order, send_order, n_kept, vectors, dense, half, before, handed, *refs):
    width, chunks = vectors.shape[2], half.shape[0]
    kept, own, tile_out = refs[:n_kept], refs[n_kept], refs[-1]
    sends = dict(zip(send_order, refs[n_kept + 1 : -1]))
    count = own.shape[0]
    rows = count * width // LANES
    sums = None
    for m in range(chunks):
        total = half[m] + dots(pb, order, vectors, dense, m, width)
        probes = (handed[m - n_kept] if m >= n_kept else kept[m][...]).astype(F32)
        part = jnp.sum(probes * total, axis=1, keepdims=True)
        sums = part if sums is None else sums + part
        if m == 0:
            own[...] = total
        else:
            put_halves(sends[m], 0, total.astype(BF16))
    both = before[...][:2] + jnp.concatenate([jnp.zeros((1, LANES), F32), 2.0 * as_row(sums)], axis=0)
    tile_out[...] = jnp.concatenate([both, jnp.zeros((6, LANES), F32)], axis=0)
    high, low = two_parts(both)
    tile = jnp.concatenate([high, low, jnp.zeros((12, LANES), F32)], axis=0).astype(BF16)
    for send in sends.values():
        send[pl.ds(rows, 16), :] = tile


def cast_kernel(t_cur, probes, rounded_probes, *refs):
    *outs, held, sems = refs
    copies = [pltpu.make_async_copy(x, held.at[n], sems.at[n]) for n, x in enumerate((t_cur, probes))]
    for copy in copies:
        copy.start()
    copies[0].wait()
    for out in outs:
        out[...] = held[0].astype(BF16)
    copies[1].wait()
    rounded_probes[...] = held[1].astype(BF16)


def gathered(own, received):
    count, width = own.shape
    total = own[...]
    for r in received:
        total = total + get_halves(r, 0, count, width).astype(F32)
    return total


def next_kernel(n_col, own, *refs):
    received, (prev, cur, probes, tile, *outs) = refs[: n_col - 1], refs[n_col - 1 :]
    value = 2.0 * gathered(own, received) - prev[...]
    for out in outs:
        out[...] = value.astype(BF16)
    ahead = as_row(jnp.sum(probes[...] * value, axis=1, keepdims=True))
    back = as_row(jnp.sum(probes[...] * cur[...], axis=1, keepdims=True))
    tile[...] = jnp.concatenate([ahead, -back, jnp.zeros((6, LANES), F32)], axis=0)


def value_kernel(n_col, own, *refs):
    received, (prev, out) = refs[: n_col - 1], refs[n_col - 1 :]
    out[...] = 2.0 * gathered(own, received) - prev[...]


def tile_kernel(start, n_received, mine, *refs):
    received, outs = refs[:n_received], refs[n_received:]
    total = mine[...]
    for r in received:
        t = r[pl.ds(start, 16), :].astype(F32)
        total = total + jnp.concatenate([t[0:2] + t[2:4], jnp.zeros((6, LANES), F32)], axis=0)
    for out in outs:
        out[...] = total


def last_kernel(n_col, coeffs, own, *refs):
    received = refs[: n_col - 1]
    prev, t_next, accum, t_after, accum_out = refs[n_col - 1 :]
    value = 2.0 * gathered(own, received) - prev[...]
    t_after[...] = value
    accum_out[...] = accum[...] + coeffs[0] * t_next[...] + coeffs[1] * value


def local(n_row, n_col, blocks, block_rows, block_cols, block_count, probes, t_prev, t_cur, accum, coeffs):
    n_slots, bs = blocks.shape[2], blocks.shape[-1]
    count, width = t_cur.shape
    pb = width // bs
    total_rows = width * n_row * n_col
    dense_bytes = n_row * n_col * width * width * 2
    params = pltpu.CompilerParams(vmem_limit_bytes=min(60 * 1024 * 1024, 3 * dense_bytes))
    barrier = lax.optimization_barrier

    def swap(x, axis, k):
        n = n_row if axis == "row" else n_col
        return lax.ppermute(x, axis, [(i, i ^ k) for i in range(n)])

    def call(kernel, out_shape, in_specs, name, **more):
        one = not isinstance(out_shape, list)
        return pl.pallas_call(
            kernel,
            out_shape=out_shape,
            in_specs=in_specs,
            out_specs=VMEM if one else [VMEM] * len(out_shape),
            compiler_params=params,
            name=name,
            **more,
        )

    def in_hbm(x):
        return pltpu.with_memory_space_constraint(x, pltpu.HBM)

    def shape(*dims, dtype=F32):
        return jax.ShapeDtypeStruct(dims, dtype)

    group = 8
    dense = call(
        functools.partial(place_kernel, pb, group),
        shape(n_row * pb, n_col * width, bs, dtype=BF16),
        [SMEM] + [HBM] * 3,
        "place",
        scratch_shapes=[
            pltpu.VMEM((n_slots, bs, bs), BF16),
            pltpu.SMEM(block_rows.shape, jnp.int32),
            pltpu.SMEM(block_cols.shape, jnp.int32),
            pltpu.SemaphoreType.DMA((n_slots // group,)),
            pltpu.SemaphoreType.DMA((2,)),
        ],
    )(block_count, *(in_hbm(x) for x in (block_rows, block_cols, blocks)))

    far = list(range(n_row - 2, 0, -2))
    orders = [FAR_A, FAR_C, FAR_M] if n_row == 8 else [far] * 3
    n_out = len(far) + 1
    def gather(far, v, *copies):
        return [v] + [swap(copy, "row", k ^ 1) for copy, k in zip(copies, far)]

    rows = width // LANES * count

    def multiply(split, early, late, order, kernel, send_order, carried, extra_rows, tail_shapes, name):
        other_early, other_late = swap(early, "row", 1), swap(late, "row", 1)
        sums, others_order = shape(n_col, count, width), [k ^ 1 for k in order]
        n_early = early.shape[0]
        first, second = (early, jnp.concatenate([late, other_early])) if split else (jnp.concatenate([early, late]), other_early)
        n_first = first.shape[0]
        both = order + others_order
        most = call(
            functools.partial(start_kernel, pb, both[:n_first]), sums, [VMEM] * 2, name + "_start"
        )(first, dense)
        most = call(
            functools.partial(more_kernel, pb, both[n_first : len(order) + n_early]),
            sums,
            [VMEM] * 3,
            name + "_more",
        )(second, dense, most)
        outs = [shape(count, width)]
        outs += [shape(rows + extra_rows.get(m, 0), LANES, dtype=BF16) for m in send_order] + tail_shapes
        return call(
            functools.partial(kernel, pb, others_order[n_early:], send_order),
            outs,
            [VMEM] * (3 + len(carried)),
            name + "_end",
        )(other_late, dense, most, *carried)

    first_order = second_order = list(range(1, n_col))
    if n_col == 4:
        first_order, second_order = ORDER1, ORDER2

    def exchange(sends, order):
        return [swap(send, "col", m) for m, send in zip(order, sends)]

    rounded_probes, *v = call(
        cast_kernel,
        [shape(count, width, dtype=BF16)] * (1 + n_out),
        [HBM] * 2,
        "cast",
        scratch_shapes=[pltpu.VMEM((2, count, width), F32), pltpu.SemaphoreType.DMA((2,))],
    )(in_hbm(t_cur), in_hbm(probes))
    got = gather(orders[0], *v)
    kept, k = [rounded_probes], 1
    while 2 * k < n_col:
        kept += [swap(piece, "col", k) for piece in kept]
        k *= 2
    got[-1], dense = barrier((got[-1], dense))
    own, *sends = multiply(
        False,
        jnp.stack(got[:-1]),
        got[-1][None],
        [0] + [k ^ 1 for k in orders[0]],
        end_kernel,
        first_order,
        [],
        {},
        [],
        "first",
    )
    sends, kept = barrier((sends, kept))
    handed = swap(jnp.stack(kept), "col", k)
    received = exchange(sends, first_order)
    tile, *rounded = call(
        functools.partial(next_kernel, n_col),
        [shape(8, LANES)] + [shape(count, width, dtype=BF16)] * n_out,
        [VMEM] * (n_col + 3),
        "next",
    )(own, *received, t_prev, t_cur, probes)
    t_next = call(
        functools.partial(value_kernel, n_col), shape(count, width), [VMEM] * (n_col + 1), "value"
    )(own, *received, t_prev)

    got = gather(orders[1], *rounded)
    got[1], t_next, handed = barrier((got[1], t_next, handed))
    own, *sends, mine = multiply(
        True,
        jnp.stack(got[:2]),
        jnp.stack(got[2:]),
        [0] + [k ^ 1 for k in orders[1]],
        lambda *a: end_moment_kernel(*a[:3], len(kept), *a[3:]),
        second_order,
        [tile, handed, probes] + kept[1:],
        dict.fromkeys(second_order, 16),
        [shape(8, LANES)],
        "second",
    )
    received = exchange(sends, second_order)
    total, *tiles = call(
        functools.partial(tile_kernel, rows, n_col - 1), [shape(8, LANES)] * n_out, [VMEM] * n_col, "sums"
    )(mine, *received)
    t_after, accum_out = call(
        functools.partial(last_kernel, n_col),
        [shape(count, width), shape(count, width)],
        [SMEM] + [VMEM] * (n_col + 3),
        "last",
    )(coeffs, own, *received, t_cur, t_next, accum)

    got = [swap(tile, "row", k ^ 1) for tile, k in zip(tiles, orders[2])]
    got, t_after, accum_out = barrier((got, t_after, accum_out))
    for one in got:
        total = total + one
    scale = float(total_rows) ** (-0.5)
    other = swap(total, "row", 1)
    moments = (total[:2, :count] + other[:2, :count]) * scale
    return (t_next, t_after, accum_out, moments)


def solution(mesh):
    vector = P(None, ("row", "col"))
    return jax.shard_map(
        functools.partial(local, mesh.shape["row"], mesh.shape["col"]),
        mesh=mesh,
        in_specs=(
            P("row", "col", None, None, None),
            P("row", "col", None),
            P("row", "col", None),
            P("row", "col"),
            vector,
            vector,
            vector,
            vector,
            P(),
        ),
        out_specs=(vector, vector, vector, P()),
        check_vma=False,
    )
```

```python
import functools

import jax
import jax.numpy as jnp
from jax import lax
from jax.experimental import pallas as pl
from jax.experimental.pallas import tpu as pltpu
from jax.sharding import PartitionSpec as P

VMEM = pl.BlockSpec(memory_space=pltpu.VMEM)
SMEM = pl.BlockSpec(memory_space=pltpu.SMEM)
HBM = pl.BlockSpec(memory_space=pltpu.HBM)
CONTRACT_LAST = (((1,), (1,)), ((), ()))
F32, BF16 = jnp.float32, jnp.bfloat16
LANES = 128
ORDER1 = [3, 2, 1]
ORDER2 = [2, 3, 1]
FAR_A, FAR_C, FAR_M = [6, 4, 2], [6, 4, 2], [6, 4, 2]


def place_kernel(pb, group, count, rows_in, cols_in, blocks, dense, held, rows, cols, sems, own_sems):
    r, c = lax.axis_index("row"), lax.axis_index("col")
    bs = blocks.shape[-1]
    groups = held.shape[0] // group

    def fetch(g):
        span = pl.ds(g * group, group)
        return pltpu.make_async_copy(blocks.at[0, 0, span], held.at[span], sems.at[g])

    names = (
        pltpu.make_async_copy(rows_in, rows, own_sems.at[0]),
        pltpu.make_async_copy(cols_in, cols, own_sems.at[1]),
    )
    for copy in names:
        copy.start()
    for g in range(groups):
        fetch(g).start()
    dense[...] = jnp.zeros_like(dense)
    for copy in names:
        copy.wait()
    live = count[0, 0]

    def put(slot):
        @pl.when(slot < live)
        def _():
            column, line = cols[0, 0, slot] ^ (r * pb), rows[0, 0, slot] ^ (c * pb)
            dense[column, pl.ds(pl.multiple_of(line * bs, bs), bs), :] = held[slot]

    for g in range(groups):
        fetch(g).wait()
        for n in range(group):
            put(g * group + n)


def dots(pb, order, vectors, dense, m, width):
    total = None
    for h, k in enumerate(order):
        w = jnp.concatenate([dense[k * pb + s, pl.ds(m * width, width), :] for s in range(pb)], axis=1)
        part = lax.dot_general(vectors[h], w, CONTRACT_LAST, preferred_element_type=F32)
        total = part if total is None else total + part
    return total


def start_kernel(pb, order, vectors, dense, out):
    width = vectors.shape[2]
    for m in range(out.shape[0]):
        out[m] = dots(pb, order, vectors, dense, m, width)


def more_kernel(pb, order, vectors, dense, before, out):
    width = vectors.shape[2]
    for m in range(out.shape[0]):
        out[m] = before[m] + dots(pb, order, vectors, dense, m, width)


def as_row(column):
    n = column.shape[0]
    shape = (n, LANES)
    here = lax.broadcasted_iota(jnp.int32, shape, 0) == lax.broadcasted_iota(jnp.int32, shape, 1)
    return jnp.sum(jnp.where(here, column, 0.0), axis=0, keepdims=True)


def two_parts(x):
    high = x.astype(BF16).astype(F32)
    return high, x - high


def put_halves(ref, start, value):
    count = value.shape[0]
    for s in range(value.shape[1] // LANES):
        ref[pl.ds(start + s * count, count), :] = value[:, s * LANES : (s + 1) * LANES]


def get_halves(ref, start, count, width):
    return jnp.concatenate(
        [ref[pl.ds(start + s * count, count), :] for s in range(width // LANES)], axis=1
    )


def end_kernel(pb, order, send_order, vectors, dense, before, own, *refs):
    width, sends = vectors.shape[2], dict(zip(send_order, refs))
    for m in range(before.shape[0]):
        total = before[m] + dots(pb, order, vectors, dense, m, width)
        if m == 0:
            own[...] = total
        else:
            put_halves(sends[m], 0, total.astype(BF16))


def end_moment_kernel(pb, order, send_order, n_kept, vectors, dense, half, before, handed, *refs):
    width, chunks = vectors.shape[2], half.shape[0]
    kept, own, tile_out = refs[:n_kept], refs[n_kept], refs[-1]
    sends = dict(zip(send_order, refs[n_kept + 1 : -1]))
    count = own.shape[0]
    rows = count * width // LANES
    sums = None
    for m in range(chunks):
        total = half[m] + dots(pb, order, vectors, dense, m, width)
        probes = (handed[m - n_kept] if m >= n_kept else kept[m][...]).astype(F32)
        part = jnp.sum(probes * total, axis=1, keepdims=True)
        sums = part if sums is None else sums + part
        if m == 0:
            own[...] = total
        else:
            put_halves(sends[m], 0, total.astype(BF16))
    both = before[...][:2] + jnp.concatenate([jnp.zeros((1, LANES), F32), 2.0 * as_row(sums)], axis=0)
    tile_out[...] = jnp.concatenate([both, jnp.zeros((6, LANES), F32)], axis=0)
    high, low = two_parts(both)
    tile = jnp.concatenate([high, low, jnp.zeros((12, LANES), F32)], axis=0).astype(BF16)
    for send in sends.values():
        send[pl.ds(rows, 16), :] = tile


def cast_kernel(t_cur, probes, rounded_probes, *refs):
    *outs, held, sems = refs
    copies = [pltpu.make_async_copy(x, held.at[n], sems.at[n]) for n, x in enumerate((t_cur, probes))]
    for copy in copies:
        copy.start()
    copies[0].wait()
    for out in outs:
        out[...] = held[0].astype(BF16)
    copies[1].wait()
    rounded_probes[...] = held[1].astype(BF16)


def gathered(own, received):
    count, width = own.shape
    total = own[...]
    for r in received:
        total = total + get_halves(r, 0, count, width).astype(F32)
    return total


def next_kernel(n_col, own, *refs):
    received, (prev, *outs) = refs[: n_col - 1], refs[n_col - 1 :]
    value = 2.0 * gathered(own, received) - prev[...]
    for out in outs:
        out[...] = value.astype(BF16)


def value_kernel(n_col, own, *refs):
    received, (prev, cur, probes, out, tile) = refs[: n_col - 1], refs[n_col - 1 :]
    value = 2.0 * gathered(own, received) - prev[...]
    out[...] = value
    ahead = as_row(jnp.sum(probes[...] * value, axis=1, keepdims=True))
    back = as_row(jnp.sum(probes[...] * cur[...], axis=1, keepdims=True))
    tile[...] = jnp.concatenate([ahead, -back, jnp.zeros((6, LANES), F32)], axis=0)


def tile_kernel(start, n_received, mine, *refs):
    received, outs = refs[:n_received], refs[n_received:]
    total = mine[...]
    for r in received:
        t = r[pl.ds(start, 16), :].astype(F32)
        total = total + jnp.concatenate([t[0:2] + t[2:4], jnp.zeros((6, LANES), F32)], axis=0)
    for out in outs:
        out[...] = total


def last_kernel(n_col, coeffs, own, *refs):
    received = refs[: n_col - 1]
    prev, t_next, accum, t_after, accum_out = refs[n_col - 1 :]
    value = 2.0 * gathered(own, received) - prev[...]
    t_after[...] = value
    accum_out[...] = accum[...] + coeffs[0] * t_next[...] + coeffs[1] * value


def local(n_row, n_col, blocks, block_rows, block_cols, block_count, probes, t_prev, t_cur, accum, coeffs):
    n_slots, bs = blocks.shape[2], blocks.shape[-1]
    count, width = t_cur.shape
    pb = width // bs
    total_rows = width * n_row * n_col
    dense_bytes = n_row * n_col * width * width * 2
    params = pltpu.CompilerParams(vmem_limit_bytes=min(60 * 1024 * 1024, 3 * dense_bytes))
    barrier = lax.optimization_barrier

    def swap(x, axis, k):
        n = n_row if axis == "row" else n_col
        return lax.ppermute(x, axis, [(i, i ^ k) for i in range(n)])

    def call(kernel, out_shape, in_specs, name, **more):
        one = not isinstance(out_shape, list)
        return pl.pallas_call(
            kernel,
            out_shape=out_shape,
            in_specs=in_specs,
            out_specs=VMEM if one else [VMEM] * len(out_shape),
            compiler_params=params,
            name=name,
            **more,
        )

    def in_hbm(x):
        return pltpu.with_memory_space_constraint(x, pltpu.HBM)

    def shape(*dims, dtype=F32):
        return jax.ShapeDtypeStruct(dims, dtype)

    group = 8
    dense = call(
        functools.partial(place_kernel, pb, group),
        shape(n_row * pb, n_col * width, bs, dtype=BF16),
        [SMEM] + [HBM] * 3,
        "place",
        scratch_shapes=[
            pltpu.VMEM((n_slots, bs, bs), BF16),
            pltpu.SMEM(block_rows.shape, jnp.int32),
            pltpu.SMEM(block_cols.shape, jnp.int32),
            pltpu.SemaphoreType.DMA((n_slots // group,)),
            pltpu.SemaphoreType.DMA((2,)),
        ],
    )(block_count, *(in_hbm(x) for x in (block_rows, block_cols, blocks)))

    far = list(range(n_row - 2, 0, -2))
    orders = [FAR_A, FAR_C, FAR_M] if n_row == 8 else [far] * 3
    n_out = len(far) + 1
    def gather(far, v, *copies):
        return [v] + [swap(copy, "row", k ^ 1) for copy, k in zip(copies, far)]

    rows = width // LANES * count

    def multiply(split, early, late, order, kernel, send_order, carried, extra_rows, tail_shapes, name):
        other_early, other_late = swap(early, "row", 1), swap(late, "row", 1)
        sums, others_order = shape(n_col, count, width), [k ^ 1 for k in order]
        n_early = early.shape[0]
        first, second = (early, jnp.concatenate([late, other_early])) if split else (jnp.concatenate([early, late]), other_early)
        n_first = first.shape[0]
        both = order + others_order
        most = call(
            functools.partial(start_kernel, pb, both[:n_first]), sums, [VMEM] * 2, name + "_start"
        )(first, dense)
        most = call(
            functools.partial(more_kernel, pb, both[n_first : len(order) + n_early]),
            sums,
            [VMEM] * 3,
            name + "_more",
        )(second, dense, most)
        outs = [shape(count, width)]
        outs += [shape(rows + extra_rows.get(m, 0), LANES, dtype=BF16) for m in send_order] + tail_shapes
        return call(
            functools.partial(kernel, pb, others_order[n_early:], send_order),
            outs,
            [VMEM] * (3 + len(carried)),
            name + "_end",
        )(other_late, dense, most, *carried)

    first_order = second_order = list(range(1, n_col))
    if n_col == 4:
        first_order, second_order = ORDER1, ORDER2

    def exchange(sends, order):
        return [swap(send, "col", m) for m, send in zip(order, sends)]

    rounded_probes, *v = call(
        cast_kernel,
        [shape(count, width, dtype=BF16)] * (1 + n_out),
        [HBM] * 2,
        "cast",
        scratch_shapes=[pltpu.VMEM((2, count, width), F32), pltpu.SemaphoreType.DMA((2,))],
    )(in_hbm(t_cur), in_hbm(probes))
    got = gather(orders[0], *v)
    kept, k = [rounded_probes], 1
    while 2 * k < n_col:
        kept += [swap(piece, "col", k) for piece in kept]
        k *= 2
    got[-1], dense = barrier((got[-1], dense))
    own, *sends = multiply(
        False,
        jnp.stack(got[:-1]),
        got[-1][None],
        [0] + [k ^ 1 for k in orders[0]],
        end_kernel,
        first_order,
        [],
        {},
        [],
        "first",
    )
    sends, kept = barrier((sends, kept))
    handed = swap(jnp.stack(kept), "col", k)
    received = exchange(sends, first_order)
    rounded = call(
        functools.partial(next_kernel, n_col),
        [shape(count, width, dtype=BF16)] * n_out,
        [VMEM] * (n_col + 1),
        "next",
    )(own, *received, t_prev)
    t_next, tile = call(
        functools.partial(value_kernel, n_col),
        [shape(count, width), shape(8, LANES)],
        [VMEM] * (n_col + 3),
        "value",
    )(own, *received, t_prev, t_cur, probes)

    got = gather(orders[1], *rounded)
    got[1], t_next, handed = barrier((got[1], t_next, handed))
    own, *sends, mine = multiply(
        True,
        jnp.stack(got[:2]),
        jnp.stack(got[2:]),
        [0] + [k ^ 1 for k in orders[1]],
        lambda *a: end_moment_kernel(*a[:3], len(kept), *a[3:]),
        second_order,
        [tile, handed, probes] + kept[1:],
        dict.fromkeys(second_order, 16),
        [shape(8, LANES)],
        "second",
    )
    received = exchange(sends, second_order)
    total, *tiles = call(
        functools.partial(tile_kernel, rows, n_col - 1), [shape(8, LANES)] * n_out, [VMEM] * n_col, "sums"
    )(mine, *received)
    t_after, accum_out = call(
        functools.partial(last_kernel, n_col),
        [shape(count, width), shape(count, width)],
        [SMEM] + [VMEM] * (n_col + 3),
        "last",
    )(coeffs, own, *received, t_cur, t_next, accum)

    got = [swap(tile, "row", k ^ 1) for tile, k in zip(tiles, orders[2])]
    got, t_after, accum_out = barrier((got, t_after, accum_out))
    for one in got:
        total = total + one
    total = total + swap(total, "row", 1)
    moments = total[:2, :count] * float(total_rows) ** (-0.5)
    return (t_next, t_after, accum_out, moments)


def solution(mesh):
    vector = P(None, ("row", "col"))
    return jax.shard_map(
        functools.partial(local, mesh.shape["row"], mesh.shape["col"]),
        mesh=mesh,
        in_specs=(
            P("row", "col", None, None, None),
            P("row", "col", None),
            P("row", "col", None),
            P("row", "col"),
            vector,
            vector,
            vector,
            vector,
            P(),
        ),
        out_specs=(vector, vector, vector, P()),
        check_vma=False,
    )
```
